32 devices in a mesh: task: 4 (over x, core), wide: 8 (over z, y).
Axes of the slice: x: 2, y: 2, z: 4, core: 2. Of those that a mesh axis runs over, the one named last changes fastest.
Arguments:
- tokens: bfloat16 [2, 4, 512, 8, 512], P(None, 'task', None, 'wide'), may hold values from -6 to 6
- cotangent: bfloat16 [2, 4, 512, 8, 512], P(None, 'task', None, 'wide'), may hold values from -6 to 6
- sample_count: int32 [2, 4], P(None, 'task'), may hold values from 64 to 512, as said below
- feature_count: int32 [2, 4], P(None, 'task'), may hold values from 2 to 8, as said below
- sample_gain: bfloat16 [512], P(('task', 'wide')), may hold values from 0.099609375 to 1.8984375
- sample_shift: bfloat16 [512], P(('task', 'wide')), may hold values from -3 to 3
- sample_qkv: bfloat16 [512, 1536], P(('task', 'wide')), may hold values from -0.25 to 0.25
- sample_proj: bfloat16 [512, 512], P(('task', 'wide')), may hold values from -3 to 3
- sample_bias: bfloat16 [512], P(('task', 'wide')), may hold values from -2 to 2
- feature_gain: bfloat16 [512], P(('task', 'wide')), may hold values from 0.099609375 to 1.8984375
- feature_shift: bfloat16 [512], P(('task', 'wide')), may hold values from -3 to 3
- feature_qkv: bfloat16 [512, 1536], P(('task', 'wide')), may hold values from -0.25 to 0.25
- feature_proj: bfloat16 [512, 512], P(('task', 'wide')), may hold values from -0.375 to 0.375
- feature_bias: bfloat16 [512], P(('task', 'wide')), may hold values from -2 to 2
- mlp_gain: bfloat16 [512], P(('task', 'wide')), may hold values from 0.099609375 to 1.8984375
- mlp_shift: bfloat16 [512], P(('task', 'wide')), may hold values from -3 to 3
- up_weight: bfloat16 [512, 2048], P(('task', 'wide')), may hold values from -0.25 to 0.25
- up_bias: bfloat16 [2048], P(('task', 'wide')), may hold values from -3 to 3
- down_weight: bfloat16 [2048, 512], P(('task', 'wide')), may hold values from -0.125 to 0.125
- down_bias: bfloat16 [512], P(('task', 'wide')), may hold values from -2 to 2
Outputs:
- output: bfloat16 [2, 4, 512, 8, 512], P(None, 'task', None, 'wide')
- input_grad: bfloat16 [2, 4, 512, 8, 512], P(None, 'task', None, 'wide')
- grad_sample_gain: float32 [512], P(('task', 'wide'))
- grad_sample_shift: float32 [512], P(('task', 'wide'))
- grad_sample_qkv: float32 [512, 1536], P(('task', 'wide'))
- grad_sample_proj: float32 [512, 512], P(('task', 'wide'))
- grad_sample_bias: float32 [512], P(('task', 'wide'))
- grad_feature_gain: float32 [512], P(('task', 'wide'))
- grad_feature_shift: float32 [512], P(('task', 'wide'))
- grad_feature_qkv: float32 [512, 1536], P(('task', 'wide'))
- grad_feature_proj: float32 [512, 512], P(('task', 'wide'))
- grad_feature_bias: float32 [512], P(('task', 'wide'))
- grad_mlp_gain: float32 [512], P(('task', 'wide'))
- grad_mlp_shift: float32 [512], P(('task', 'wide'))
- grad_up_weight: float32 [512, 2048], P(('task', 'wide'))
- grad_up_bias: float32 [2048], P(('task', 'wide'))
- grad_down_weight: float32 [2048, 512], P(('task', 'wide'))
- grad_down_bias: float32 [512], P(('task', 'wide'))
The draws below stay inside these ranges and needn't reach their ends.
Inputs may be any that keep to these rules, and one draw needn't show every extreme that they name: `sample_count`: for every task index, one of the micro-batches (drawn) holds a task with all 512 samples real. `feature_count`: for every task index, one of the micro-batches (drawn) holds a task with all 8 features real.
All inputs are finite; a program needn't handle non-finite values.
Results may differ from the reference program's by a relative error of at most 0.014.
Values may be sent and summed in bfloat16 or wider, within the bound.
A program may use at most 192 MiB of HBM per device.

```python
import math
import jax
import jax.numpy as jnp
from jax import lax

D = 512
HEADS = 8
HEAD_SIZE = 64
FF = 2048
SAMPLES = 512
MICRO = 2
FEATURES = 8
TASKS = 4


def pick_full(key, lowest, highest):
    first_key, second_key = jax.random.split(key)
    chosen = jax.random.randint(first_key, (TASKS,), 0, MICRO)
    drawn = jax.random.randint(second_key, (MICRO, TASKS), lowest, highest + 1)
    is_full = jnp.arange(MICRO)[:, None] == chosen[None, :]
    return jnp.where(is_full, highest, drawn).astype(jnp.int32)


def draw_sample_count(key, part):
    key = jax.random.fold_in(key, 3)
    return pick_full(key, max(2, SAMPLES // 8), SAMPLES)


def draw_feature_count(key, part):
    key = jax.random.fold_in(key, 7)
    return pick_full(key, max(1, FEATURES // 4), FEATURES)


def levels(key, dims, cuts, low, largest):
    def one(position, parts):
        draws = jax.random.uniform(jax.random.fold_in(jax.random.fold_in(key, 6), position), (parts,), jnp.float32, low / len(cuts), largest / len(cuts))
        return jnp.repeat(jnp.exp(draws), dims[position] // parts).reshape((-1,) + (1,) * (len(dims) - position - 1))

    loudness = one(*cuts[0])
    for cut in cuts[1:]:
        loudness = loudness * one(*cut)
    return loudness


def normal_values(rng, shape, deviation, limit, cuts=(), held_as=jnp.bfloat16):
    values = jax.random.normal(rng, shape, jnp.float32) * deviation
    if len(cuts) > 0:
        values = levels(rng, shape, cuts, -0.22, 0.18) * values
    return jnp.clip(values, min=-limit, max=limit).astype(held_as)


def setup_inputs(seed: int = 0) -> dict:
    splits = jax.random.split(jax.random.key(seed), 21)
    return {
        "tokens": normal_values(splits[0], (MICRO, TASKS, SAMPLES, FEATURES, D), 1.0, 6.0, ((1, 4), (3, 8))),
        "cotangent": normal_values(splits[1], (MICRO, TASKS, SAMPLES, FEATURES, D), 1.0, 6.0, ((1, 4), (3, 8))),
        "sample_count": draw_sample_count(jax.random.fold_in(splits[20], 71), 0),
        "feature_count": draw_feature_count(jax.random.fold_in(splits[20], 71), 0),
        "sample_gain": jnp.clip(1.0 + 0.18 * jax.random.normal(splits[4], (D,), jnp.float32), 0.099609375, 1.8984375).astype(jnp.bfloat16),
        "sample_shift": normal_values(splits[5], (D,), 0.5, 3.0, ((0, 32),)),
        "sample_qkv": normal_values(splits[6], (D, 3 * D), D ** -0.5, 0.25, ((0, 32),)),
        "sample_proj": normal_values(splits[7], (D, D), (4 * D // SAMPLES) ** -0.5, 3.0, ((0, 32),)),
        "sample_bias": normal_values(splits[8], (D,), 0.3, 2.0, ((0, 32),)),
        "feature_gain": jnp.clip(1.0 + 0.18 * jax.random.normal(splits[9], (D,), jnp.float32), 0.099609375, 1.8984375).astype(jnp.bfloat16),
        "feature_shift": normal_values(splits[10], (D,), 0.5, 3.0, ((0, 32),)),
        "feature_qkv": normal_values(splits[11], (D, 3 * D), D ** -0.5, 0.25, ((0, 32),)),
        "feature_proj": normal_values(splits[12], (D, D), (4 * D // FEATURES) ** -0.5, 0.375, ((0, 32),)),
        "feature_bias": normal_values(splits[13], (D,), 0.3, 2.0, ((0, 32),)),
        "mlp_gain": jnp.clip(1.0 + 0.18 * jax.random.normal(splits[14], (D,), jnp.float32), 0.099609375, 1.8984375).astype(jnp.bfloat16),
        "mlp_shift": normal_values(splits[15], (D,), 0.5, 3.0, ((0, 32),)),
        "up_weight": normal_values(splits[16], (D, FF), D ** -0.5, 0.25, ((0, 32),)),
        "up_bias": normal_values(splits[17], (FF,), 0.5, 3.0, ((0, 32),)),
        "down_weight": normal_values(splits[18], (FF, D), FF ** -0.5, 0.125, ((0, 32),)),
        "down_bias": normal_values(splits[19], (D,), 0.3, 2.0, ((0, 32),)),
    }


highest = lax.Precision.HIGHEST
epsilon = 1e-05
masked_score = -1e+30

@jax.custom_vjp
def low(v):
    return lax.optimization_barrier(v.astype(jnp.bfloat16)).astype(jnp.float32)

@jax.custom_vjp
def low_back(v):
    return v

def low_keep(v):
    return (low(v), None)

def low_pass(kept, grad):
    return (grad,)

def back_keep(v):
    return (v, None)

def back_low(kept, grad):
    return (low(grad),)
low.defvjp(low_keep, low_pass)
low_back.defvjp(back_keep, back_low)

def layer_norm(values, norm_gain, norm_shift):
    centred = values - lax.optimization_barrier(jnp.mean(values, -1, keepdims=True))
    variance = lax.optimization_barrier(jnp.mean(centred * centred, -1, keepdims=True))
    return centred * lax.rsqrt(variance + epsilon) * norm_gain + norm_shift

def attention_block(pieces):
    queries, keys, values_in, key_valid = pieces
    score_scale = HEAD_SIZE ** (-0.5)
    raw_scores = jnp.einsum('nlhe,nmhe->nhlm', queries, keys, precision=highest)
    scores = low_back(raw_scores * score_scale)
    scores = jnp.where(key_valid[:, None, None, :], scores, masked_score)
    probabilities = low(jax.nn.softmax(scores, axis=-1))
    return jnp.einsum('nhlm,nmhe->nlhe', probabilities, values_in, precision=highest)

def mixer(stream, key_valid, weights):
    norm_gain, norm_shift, packed_weight, proj_weight, proj_bias = weights
    sequences, length, model_width = stream.shape
    normed = low(layer_norm(stream, norm_gain, norm_shift))
    packed = low_back(low(jnp.einsum('nld,de->nle', normed, packed_weight, precision=highest)))
    split_qkv = packed.reshape(sequences, length, 3, HEADS, HEAD_SIZE)
    per_block = math.gcd(sequences, max(1, 4096 // length))
    blocks = sequences // per_block

    def blocked(array):
        return array.reshape((blocks, per_block) + array.shape[1:])
    attended = lax.map(jax.checkpoint(attention_block), (blocked(split_qkv[:, :, 0]), blocked(split_qkv[:, :, 1]), blocked(split_qkv[:, :, 2]), blocked(key_valid)))
    attended = low_back(low(attended.reshape(sequences, length, model_width)))
    branch = low_back(jnp.einsum('nld,de->nle', attended, proj_weight, precision=highest) + proj_bias)
    return stream + branch

def layer(stream, samples, features, weights):
    length, columns_count, model_width = stream.shape
    by_feature = jnp.swapaxes(stream, 0, 1)
    sample_valid = jnp.broadcast_to(jnp.arange(length) < samples, (columns_count, length))
    after_first = low_back(low(mixer(by_feature, sample_valid, weights[0:5])))
    by_sample = jnp.swapaxes(after_first, 0, 1)
    feature_valid = jnp.broadcast_to(jnp.arange(columns_count) < features, (length, columns_count))
    after_second = mixer(by_sample, feature_valid, weights[5:10])
    norm_gain, norm_shift, up_matrix, up_vector, down_matrix, down_vector = weights[10:16]
    normed = low(layer_norm(after_second, norm_gain, norm_shift))
    raised = low_back(jnp.einsum('nld,df->nlf', normed, up_matrix, precision=highest) + up_vector)
    active = low(jax.nn.gelu(raised, approximate=False))
    branch = low_back(jnp.einsum('nlf,fd->nld', active, down_matrix, precision=highest) + down_vector)
    return after_second + branch

def reference(tokens, cotangent, sample_count, feature_count, sample_gain, sample_shift, sample_qkv, sample_proj, sample_bias, feature_gain, feature_shift, feature_qkv, feature_proj, feature_bias, mlp_gain, mlp_shift, up_weight, up_bias, down_weight, down_bias):
    weights = tuple((item.astype(jnp.float32) for item in (sample_gain, sample_shift, sample_qkv, sample_proj, sample_bias, feature_gain, feature_shift, feature_qkv, feature_proj, feature_bias, mlp_gain, mlp_shift, up_weight, up_bias, down_weight, down_bias)))
    flat_tokens = tokens.astype(jnp.float32).reshape(MICRO * TASKS, SAMPLES, FEATURES, D)
    flat_samples = sample_count.reshape(MICRO * TASKS)
    flat_features = feature_count.reshape(MICRO * TASKS)

    def forward(inputs, params):

        def one_task(pieces):
            return layer(pieces[0], pieces[1], pieces[2], params)
        return lax.map(jax.checkpoint(one_task), (inputs, flat_samples, flat_features))
    result, pull_back = jax.vjp(forward, flat_tokens, weights)
    grad_tokens, grads = pull_back(cotangent.astype(jnp.float32).reshape(result.shape))
    whole_shape = tokens.shape
    return (result.astype(jnp.bfloat16).reshape(whole_shape), grad_tokens.astype(jnp.bfloat16).reshape(whole_shape), grads[0], grads[1], grads[2], grads[3], grads[4], grads[5], grads[6], grads[7], grads[8], grads[9], grads[10], grads[11], grads[12], grads[13], grads[14], grads[15])
```

```python
import jax
import jax.numpy as jnp
from jax import lax
from jax.experimental import pallas as pl
from jax.experimental.pallas import tpu as pltpu
from jax.sharding import PartitionSpec as P

HEADS = 8
HEAD_SIZE = 64
PAIRS = HEADS // 2
SCALE = HEAD_SIZE ** -0.5
TILE = 16
SPLIT = (2, 2, 4, 2)

epsilon = 1e-05
masked_score = -1e30
f32, bf16 = jnp.float32, jnp.bfloat16
MESH = pl.DeviceIdType.MESH
MIB = 1 << 20


def mm(a, b):
    return lax.dot_general(a, b, (((1,), (0,)), ((), ())), preferred_element_type=f32)


def mm_nt(a, b):
    return lax.dot_general(a, b, (((1,), (1,)), ((), ())), preferred_element_type=f32)


def mm_tn(a, b):
    return lax.dot_general(a, b, (((0,), (0,)), ((), ())), preferred_element_type=f32)


def flat(value):
    return value.reshape(-1, value.shape[-1])


def normed(v):
    centred = v - jnp.mean(v, -1, keepdims=True)
    scale = lax.rsqrt(jnp.mean(centred * centred, -1, keepdims=True) + epsilon)
    return centred * scale, scale


def normed_back(grad, unit, scale, gain):
    t = grad * gain
    return scale * (t - jnp.mean(t, -1, keepdims=True) - unit * jnp.mean(t * unit, -1, keepdims=True))


def over_rows(v):
    return jnp.sum(v, 0, keepdims=True)


def gelu_parts(x):
    z = jnp.abs(x) * (0.5 ** 0.5)
    t = 1.0 / (1.0 + 0.3275911 * z)
    e = jnp.exp(-z * z)
    poly = t * (0.254829592 + t * (-0.284496736 + t * (1.421413741 + t * (-1.453152027 + t * 1.061405429))))
    tail = 0.5 * poly * e
    return jnp.where(x >= 0, 1.0 - tail, tail), e


def half_mask(half):
    lane = lax.broadcasted_iota(jnp.int32, (1, 128), 1)
    return (lane < HEAD_SIZE) if half == 0 else (lane >= HEAD_SIZE)


def keep(mask, v):
    return jnp.where(mask, v, jnp.zeros_like(v))


def lanes(part, j):
    start = part * 512 + j * 128
    return pl.ds(start if isinstance(j, int) else pl.multiple_of(start, 128), 128)


def attend_pair(j, rows, bias, qkv, o, lse):
    q = qkv[rows, lanes(0, j)] * jnp.asarray(SCALE, bf16)
    k = qkv[rows, lanes(1, j)]
    v = qkv[rows, lanes(2, j)]
    total = None
    column = lax.broadcasted_iota(jnp.int32, (1, 128), 1)
    logs = lse[rows, :]
    for half in (0, 1):
        msk = half_mask(half)
        s = mm_nt(q, keep(msk, k)) + bias
        top = jnp.max(s, -1, keepdims=True)
        e = jnp.exp(s - top)
        mass = jnp.sum(e, -1, keepdims=True)
        part = mm(e.astype(bf16), keep(msk, v)) / mass
        total = part if total is None else total + part
        logs = jnp.where(column == 2 * j + half, top + jnp.log(mass), logs)
    lse[rows, :] = logs
    o[rows, lanes(0, j)] = total.astype(bf16)


def attend_pair_back(j, rows, bias, qkv, o, lse, do, dqkv):
    q = qkv[rows, lanes(0, j)] * jnp.asarray(SCALE, bf16)
    k = qkv[rows, lanes(1, j)]
    v = qkv[rows, lanes(2, j)]
    d = do[rows, lanes(0, j)]
    prod = d.astype(f32) * o[rows, lanes(0, j)].astype(f32)
    column = lax.broadcasted_iota(jnp.int32, (1, 128), 1)
    logs = lse[rows, :]
    dq = dk = dv = None
    for half in (0, 1):
        msk = half_mask(half)
        km, dm, qm = keep(msk, k), keep(msk, d), keep(msk, q)
        delta = jnp.sum(keep(msk, prod), -1, keepdims=True)
        log = jnp.sum(jnp.where(column == 2 * j + half, logs, 0.0), -1, keepdims=True)
        p = jnp.exp(mm_nt(q, km) + bias - log)
        ds = (p * (mm_nt(dm, v) - delta)).astype(bf16)
        a, b, c = mm(ds, km), mm_tn(ds, qm), mm_tn(p.astype(bf16), dm)
        dq, dk, dv = (a, b, c) if half == 0 else (dq + a, dk + b, dv + c)
    dqkv[rows, lanes(0, j)] = (dq * SCALE).astype(bf16)
    dqkv[rows, lanes(1, j)] = dk.astype(bf16)
    dqkv[rows, lanes(2, j)] = dv.astype(bf16)


def loop(n, body, unrolled=False):
    if unrolled:
        for i in range(n):
            body(i)
    else:
        def step(i, carry):
            body(i)
            return carry
        lax.fori_loop(0, n, step, 0)


def project(h, W, qkv):
    qkv[:, 0:1024] = mm(h, flat(W[0])).astype(bf16)
    qkv[:, 1024:1536] = mm(h, flat(W[1, ..., 0:512])).astype(bf16)


def out_proj(W):
    return flat(W[1, ..., 512:1024])


def put(ref, index, value, add):
    value = value.reshape(ref.at[index].shape)
    if add is False:
        ref[index] = value
    else:
        ref[index] = ref[index] + value


LEFT, RIGHT = slice(0, 512), slice(512, 1024)


class Place:
    def __init__(self, W):
        self.t, self.w, self.W = lax.axis_index("task"), lax.axis_index("wide"), W
        self.x, self.c = self.t // 2, self.t % 2
        self.z, self.y = self.w // 2, self.w % 2

    def barrier(self, direct):
        peers = [(self.t, (self.w + i) % self.W) for i in range(1, self.W)]
        if direct:
            peers += [(self.t + 1 - 2 * self.c, self.w), ((self.t + 2) % 4, self.w)]
        bar = pltpu.get_barrier_semaphore()
        for peer in peers:
            pl.semaphore_signal(bar, inc=1, device_id=peer, device_id_type=MESH)
        pl.semaphore_wait(bar, len(peers))

    def other(self, axis):
        if axis == "c":
            return (self.t + 1 - 2 * self.c, self.w)
        if axis == "x":
            return ((self.t + 2) % 4, self.w)
        return (self.t, self.w + 1 - 2 * self.y)

    def along_z(self, step):
        return (self.t, (self.w + 2 * step) % 8)


def remote(src, dst, sems, device):
    return pltpu.make_async_remote_copy(
        src_ref=src, dst_ref=dst, send_sem=sems.at[0], recv_sem=sems.at[1], device_id=device, device_id_type=MESH
    )


class Exchange:
    def __init__(self, place, src, dst, sems):
        me, W = place.w, place.W
        self.copies = []
        for i in range(W - 1, 0, -1):
            peer = (me + i) % W
            self.copies.append(remote(src(peer), dst(me), sems.at[i], (place.t, peer)))
        self.copies.append(pltpu.make_async_copy(src(me), dst(me), sems.at[0, 0]))

    def start(self):
        for copy in self.copies:
            copy.start()

    def wait(self):
        for copy in self.copies:
            copy.wait()


class Gather:
    def __init__(self, place, ref, order, sems):
        x, c, z, y = place.x, place.c, place.z, place.y
        own = ref.at[x, c, z, y]
        self.stages = [[remote(own, own, sems.at[s - 1], place.along_z(s)) for s in (1, 2, 3)]]
        line = ref.at[x, c, :, y]
        if order == "yx":
            plane = ref.at[x, c]
            self.stages.append([remote(line, line, sems.at[3], place.other("y"))])
            self.stages.append([remote(plane, plane, sems.at[4], place.other("x"))])
        else:
            plane = ref.at[:, c, :, y]
            self.stages.append([remote(line, line, sems.at[3], place.other("x"))])
            self.stages.append([remote(plane, plane, sems.at[4], place.other("y"))])
        half = ref.at[:, c]
        self.stages.append([remote(half, half, sems.at[5], place.other("c"))])

    def start(self, stage):
        for copy in self.stages[stage]:
            copy.start()

    def wait(self, stage):
        for copy in self.stages[stage]:
            copy.wait()


class SumAll:
    def __init__(self, place, slots, sems):
        peers = [[place.along_z(s) for s in (1, 2, 3)], [place.other("y")], [place.other("x")], [place.other("c")]]
        self.slots, self.stages, n = slots, [], 0
        for group in peers:
            stage = []
            for peer in group:
                stage.append((n, peer))
                n += 1
            self.stages.append(stage)
        self.copies = [
            [remote(slots.at[s], slots.at[4 + n], sems.at[n], peer) for n, peer in stage]
            for s, stage in enumerate(self.stages)
        ]

    def start(self, stage, value=None):
        if stage == 0:
            self.slots[0] = value
        for copy in self.copies[stage]:
            copy.start()

    def wait(self, stage):
        total = self.slots[stage].astype(f32)
        for copy, (n, _) in zip(self.copies[stage], self.stages[stage]):
            copy.wait()
            total = total + self.slots[4 + n].astype(f32)
        if stage < 3:
            self.slots[stage + 1] = total.astype(self.slots.dtype)
        return total


SUM_SLOTS = 10


class Scatter:
    def __init__(self, place, grad, order, bufs, sems):
        self.p, self.grad, self.order, self.sems = place, grad, order, sems
        self.recv, self.s1, self.r1, self.s2, self.r2, self.s3, self.r3 = bufs
        x, c, z, y = place.x, place.c, place.z, place.y
        self.core = remote(grad.at[:, 1 - c], self.recv, sems.at[0], place.other("c"))
        first, second = ("x", "y") if order == "xy" else ("y", "x")
        self.one = remote(self.s1, self.r1, sems.at[1], place.other(first))
        self.two = remote(self.s2, self.r2, sems.at[2], place.other(second))
        self.three = [
            remote(self.s3.at[(z + s) % 4], self.r3.at[s - 1], sems.at[2 + s], place.along_z(s)) for s in (1, 2, 3)
        ]

    def step(self, stage):
        x, c, z, y = self.p.x, self.p.c, self.p.z, self.p.y
        xy = self.order == "xy"
        sums = self.recv
        if stage == 0:
            self.core.start()
        elif stage == 1:
            self.core.wait()
            sums[...] = sums[...] + self.grad[:, c]
            self.s1[...] = (sums[1 - x] if xy else sums[:, :, 1 - y]).astype(bf16)
            self.one.start()
        elif stage == 2:
            self.one.wait()
            if xy:
                sums[x] = sums[x] + self.r1[...].astype(f32)
                self.s2[...] = sums[x, :, 1 - y].astype(bf16)
            else:
                sums[:, :, y] = sums[:, :, y] + self.r1[...].astype(f32)
                self.s2[...] = sums[1 - x, :, y].astype(bf16)
            self.two.start()
        elif stage == 3:
            self.two.wait()
            sums[x, :, y] = sums[x, :, y] + self.r2[...].astype(f32)
            self.s3[...] = sums[x, :, y].astype(bf16)
            for copy in self.three:
                copy.start()
        else:
            total = sums[x, z, y]
            for i, copy in enumerate(self.three):
                copy.wait()
                total = total + self.r3[i].astype(f32)
            return total


def scatter_bufs(rows, cols, order):
    first = (4, 2, rows, cols) if order == "xy" else (2, 4, rows, cols)
    return [
        pltpu.VMEM((2, 4, 2, rows, cols), f32),
        pltpu.VMEM(first, bf16), pltpu.VMEM(first, bf16),
        pltpu.VMEM((4, rows, cols), bf16), pltpu.VMEM((4, rows, cols), bf16),
        pltpu.VMEM((4, rows, cols), bf16), pltpu.VMEM((3, rows, cols), bf16),
    ]


ORDERS = ("yx", "xy")


VECTORS = 9


def first_kernel(direct, W, groups, *refs):
    refs = list(refs)
    take = lambda n: [refs.pop(0) for _ in range(n)]
    count, tok, cot = take(3)
    if direct:
        sq, sp, fq, fp, up, dn, small = take(7)
    else:
        A, vec_in = take(2)
    arr, cots, qkv, o, lse = take(5)
    if direct:
        vec, A, B, C, D = take(5)
    first, = take(1)
    if direct:
        slots, gsems, vsems = take(3)
    xsems, = take(1)
    p = Place(W)
    t, w = p.t, p.w
    block = lambda ref, m: lambda peer: ref.at[m, pl.ds(peer * groups, groups)]
    land = lambda ref, m: lambda me: ref.at[m, :, me]
    cot_moves = [Exchange(p, block(cot, m), land(cots, m), xsems.at[m]) for m in (0, 1)]
    first_moves = [Exchange(p, block(first, m), land(arr, m), xsems.at[2 + m]) for m in (0, 1)]
    p.barrier(direct)
    if direct:
        rank = t * 8 + w
        at = (p.x, p.c, p.z, p.y)
        A[(0, *at)] = sq[:, 0:1024]
        A[(1, *at, slice(None), LEFT)] = sq[:, 1024:1536]
        A[(1, *at, slice(None), RIGHT)] = sp[...]
        i = lax.broadcasted_iota(jnp.int32, (128, 512), 0)
        j = lax.broadcasted_iota(jnp.int32, (128, 512), 1)
        row = lax.broadcasted_iota(jnp.int32, (16, 512), 0)
        narrow = mm(small[...], (j == rank * 16 + i).astype(bf16))
        wide = mm(small[...], (j == (rank % 8) * 64 + i).astype(bf16))
        placed = jnp.where(row < VECTORS, narrow, jnp.where(row == VECTORS + rank // 8, over_rows(keep(row == VECTORS, wide)), 0.0))
        both = SumAll(p, slots, vsems)
        both.start(0, placed.astype(bf16))
        gathers = [Gather(p, ref.at[u], ORDERS[u], gsems.at[2 * n + u]) for n, ref in enumerate((A, B, C, D)) for u in (0, 1)]
        GA, GB, GC, GD = gathers[0:2], gathers[2:4], gathers[4:6], gathers[6:8]

        def go(group, stage):
            for g in group:
                if stage > 0:
                    g.wait(stage - 1)
                if stage < 4:
                    g.start(stage)

        go(GA, 0)
        for u, cols in enumerate((slice(0, 1024), slice(1024, 2048))):
            C[(u, *at)] = up[:, cols]
        B[(0, *at)] = fq[:, 0:1024]
        B[(1, *at, slice(None), LEFT)] = fq[:, 1024:1536]
        B[(1, *at, slice(None), RIGHT)] = fp[...]
        D[(0, *at)] = dn[:, 0:256]
        D[(1, *at)] = dn[:, 256:512]
        both.wait(0)
        both.start(1)
        go(GA, 1)
        cot_moves[0].start()
        go(GB, 0)
        both.wait(1)
        both.start(2)
        go(GA, 2)
        both.wait(2)
        both.start(3)
        go(GB, 1)
        go(GC, 0)
        vec[...] = both.wait(3)
        go(GA, 3)
        go(GA, 4)
    else:
        cot_moves[0].start()
    row_of = (lambda n: vec[n:n + 1, :]) if direct else (lambda n: vec_in[n:n + 1, :].astype(f32))
    valid = lax.broadcasted_iota(jnp.int32, (1, 512), 1)
    for m in (0, 1):
        bias = jnp.where(valid < count[m, 0], 0.0, masked_score)
        unit, _ = normed(tok[m].astype(f32))
        h = (unit * row_of(0) + row_of(1)).astype(bf16)
        project(h, A, qkv.at[m])
        if direct and m == 0:
            go(GB, 2)
            go(GC, 1)
            go(GD, 0)
        if m == 1:
            cot_moves[1].start()
        loop(PAIRS, lambda j: attend_pair(j, slice(None), bias, qkv.at[m], o.at[m], lse.at[m]))
        if direct and m == 0:
            go(GC, 2)
            go(GD, 1)
            go(GB, 3)
        branch = mm(o[m], out_proj(A)) + row_of(2)
        first[m] = (tok[m].astype(f32) + branch).astype(bf16).reshape(first.shape[1:])
        first_moves[m].start()
    if direct:
        go(GD, 2)
        go(GC, 3)
        go(GD, 3)
        go(GB, 4)
        go(GC, 4)
        go(GD, 4)
    for move in cot_moves + first_moves:
        move.wait()


def second_kernel(direct, W, groups, *refs):
    refs = list(refs)
    take = lambda n: [refs.pop(0) for _ in range(n)]
    count_s, count_f, tok, arr, cots, qkv_s, o_s, lse_s, vec_in, A, B, C, D = take(13)
    result, gin = take(2)
    if direct:
        out_sq, out_sp, out_fq, out_fp, out_up, out_dn = take(6)
        out_small = take(10)
    else:
        gA, gB, gC, gD, gvec_out = take(5)
    leave, gleave, grecv, vec, gvec, qkv, o, lse, stream, dout, h2, dh2 = take(12)
    dqkv, do = qkv, h2
    if direct:
        gB, gC, gD, slots, vsems, ssems = take(6)
        gA = gC
        bufs = [take(7) for _ in range(8)]
    xsems, = take(1)
    p = Place(W)
    block_rows = W * TILE
    take_out = lambda ref, m: lambda peer: ref.at[m, :, peer]
    land = lambda ref, m: lambda me: ref.at[m, pl.ds(me * groups, groups)]
    out_moves = [Exchange(p, take_out(leave, m), land(result, m), xsems.at[m]) for m in (0, 1)]
    back_moves = [Exchange(p, take_out(gleave, m), land(grecv, m), xsems.at[2 + m]) for m in (0, 1)]
    if direct:
        scatters = [
            Scatter(p, ref.at[u], ORDERS[u], bufs[2 * n + u], ssems.at[2 * n + u])
            for n, ref in enumerate((gA, gB, gC, gD)) for u in (0, 1)
        ]
        SA, SB, SC, SD = scatters[0:2], scatters[2:4], scatters[4:6], scatters[6:8]
    else:
        SA = SB = SC = SD = ()

    def go(group, stage):
        return [s.step(stage) for s in group]

    p.barrier(direct)
    for n in range(16):
        vec[n] = vec_in[n:n + 1, :].astype(f32)
    row = lambda n: vec[n]
    i = lax.broadcasted_iota(jnp.int32, (block_rows, block_rows), 0)
    j = lax.broadcasted_iota(jnp.int32, (block_rows, block_rows), 1)

    def features(m):
        add = m > 0
        bias = jnp.where((i % TILE == j % TILE) & (j // TILE < count_f[m, 0]), 0.0, masked_score)
        x = flat(arr[m]).astype(f32)
        unit, _ = normed(x)
        project((unit * row(3) + row(4)).astype(bf16), B, qkv)

        def blocks(body):
            def at_block(g):
                rows = pl.ds(pl.multiple_of(g * block_rows, block_rows), block_rows)
                loop(PAIRS, lambda n: body(n, rows), unrolled=block_rows <= 128)
            loop(groups, at_block)

        blocks(lambda n, rows: attend_pair(n, rows, bias, qkv, o, lse))
        s2 = x + mm(o[...], out_proj(B)) + row(5)
        stream[...] = s2
        unit, _ = normed(s2)
        h2[...] = (unit * row(6) + row(7)).astype(bf16)

        def chunk(n):
            half = n // 2
            cols = pl.ds(pl.multiple_of((n % 2) * 512, 512), 512)
            upw = C[half, :, :, :, :, :, cols].reshape(512, 512)
            d0 = D[0, n // 2, n % 2].reshape(512, 256)
            d1 = D[1, n // 2, n % 2].reshape(512, 256)
            g16 = flat(cots[m])
            raised = mm(h2[...], upw) + vec[VECTORS + n]
            phi, e = gelu_parts(raised)
            active = (raised * phi).astype(bf16)
            dact = mm_nt(g16[:, 0:256], d0) + mm_nt(g16[:, 256:512], d1)
            draised = (dact * (phi + raised * e * (0.5 / jnp.pi) ** 0.5)).astype(bf16)
            put(gvec, VECTORS + n, over_rows(draised.astype(f32)), add)
            a0, a1, b0 = mm(active, d0), mm(active, d1), mm_nt(draised, upw)

            @pl.when(n == 0)
            def _():
                dout[:, 0:256] = a0
                dout[:, 256:512] = a1
                dh2[...] = b0

            @pl.when(n > 0)
            def _():
                dout[:, 0:256] += a0
                dout[:, 256:512] += a1
                dh2[...] += b0

            put(gC, (half, slice(None), slice(None), slice(None), slice(None), slice(None), cols), mm_tn(h2[...], draised), add)
            put(gD, (0, n // 2, n % 2), mm_tn(active, g16[:, 0:256]), add)
            put(gD, (1, n // 2, n % 2), mm_tn(active, g16[:, 256:512]), add)

        loop(4, chunk)
        leave[m] = (stream[...] + dout[...] + row(8)).astype(bf16).reshape(leave.shape[1:])
        out_moves[m].start()
        if m == 1:
            go(SC, 0)
            go(SD, 0)
        cot = flat(cots[m]).astype(f32)
        put(gvec, 8, over_rows(cot), add)
        unit, scale = normed(stream[...])
        dh = dh2[...]
        put(gvec, 6, over_rows(dh * unit), add)
        put(gvec, 7, over_rows(dh), add)
        g2 = cot + normed_back(dh, unit, scale, row(6))
        stream[...] = g2
        gy = g2.astype(bf16)
        put(gB, (1, Ellipsis, RIGHT), mm_tn(o[...], gy), add)
        put(gvec, 5, over_rows(gy.astype(f32)), add)
        do[...] = mm_nt(gy, out_proj(B)).astype(bf16)
        blocks(lambda n, rows: attend_pair_back(n, rows, bias, qkv, o, lse, do, dqkv))
        unit, scale = normed(flat(arr[m]).astype(f32))
        h = (unit * row(3) + row(4)).astype(bf16)
        dh = mm_nt(dqkv[:, 0:1024], flat(B[0])) + mm_nt(dqkv[:, 1024:1536], flat(B[1, ..., LEFT]))
        gleave[m] = (stream[...] + normed_back(dh, unit, scale, row(3))).astype(bf16).reshape(gleave.shape[1:])
        back_moves[m].start()
        put(gvec, 3, over_rows(dh * unit), add)
        put(gvec, 4, over_rows(dh), add)
        put(gB, 0, mm_tn(h, dqkv[:, 0:1024]), add)
        put(gB, (1, Ellipsis, LEFT), mm_tn(h, dqkv[:, 1024:1536]), add)

    valid = lax.broadcasted_iota(jnp.int32, (1, 512), 1)

    def samples(m, service):
        add = m > 0
        bias = jnp.where(valid < count_s[m, 0], 0.0, masked_score)
        gy = flat(grecv[m])
        put(gA, (1, Ellipsis, RIGHT), mm_tn(o_s[m], gy), add)
        put(gvec, 2, over_rows(gy.astype(f32)), add)
        do[...] = mm_nt(gy, out_proj(A)).astype(bf16)
        service(0)
        loop(PAIRS, lambda n: attend_pair_back(n, slice(None), bias, qkv_s.at[m], o_s.at[m], lse_s.at[m], do, dqkv))
        service(1)
        unit, scale = normed(tok[m].astype(f32))
        h = (unit * row(0) + row(1)).astype(bf16)
        put(gA, 0, mm_tn(h, dqkv[:, 0:1024]), add)
        put(gA, (1, Ellipsis, LEFT), mm_tn(h, dqkv[:, 1024:1536]), add)
        if m == 1:
            go(SA, 0)
        dh = mm_nt(dqkv[:, 0:1024], flat(A[0])) + mm_nt(dqkv[:, 1024:1536], flat(A[1, ..., LEFT]))
        put(gvec, 0, over_rows(dh * unit), add)
        put(gvec, 1, over_rows(dh), add)
        gin[m] = (flat(grecv[m]).astype(f32) + normed_back(dh, unit, scale, row(0))).astype(bf16)

    features(0)
    features(1)
    go(SC, 1)
    go(SD, 1)
    go(SB, 0)
    back_moves[0].wait()
    parts = {}

    def service0(k):
        if k == 0:
            go(SC, 2)
            go(SD, 2)
            go(SB, 1)
        else:
            go(SC, 3)
            go(SD, 3)
            go(SB, 2)

    def service1(k):
        if k == 0:
            parts["C"] = go(SC, 4)
            parts["D"] = go(SD, 4)
            if direct:
                out_up[:, 0:1024], out_up[:, 1024:2048] = parts["C"]
                out_dn[:, 0:256], out_dn[:, 256:512] = parts["D"]
            go(SB, 3)
        else:
            parts["B"] = go(SB, 4)
            if direct:
                out_fq[:, 0:1024] = parts["B"][0]
                out_fq[:, 1024:1536] = parts["B"][1][:, LEFT]
                out_fp[...] = parts["B"][1][:, RIGHT]

    samples(0, service0)
    back_moves[1].wait()
    samples(1, service1)
    if direct:
        small = jnp.concatenate([gvec[n] for n in range(VECTORS + 4)] + [jnp.zeros((3, 512), f32)], 0)
        both = SumAll(p, slots, vsems)
        both.start(0, small)
        go(SA, 1)
        both.wait(0)
        both.start(1)
        go(SA, 2)
        both.wait(1)
        both.start(2)
        go(SA, 3)
        both.wait(2)
        both.start(3)
        total = both.wait(3)
        rank = p.t * 8 + p.w
        a = lax.broadcasted_iota(jnp.int32, (512, 128), 0)
        b = lax.broadcasted_iota(jnp.int32, (512, 128), 1)
        pick = lambda v, start: lax.dot_general(
            v, (a == start + b).astype(f32), (((1,), (0,)), ((), ())), precision=lax.Precision.HIGHEST, preferred_element_type=f32
        )
        own = pick(total, rank * 16)
        r16 = lax.broadcasted_iota(jnp.int32, (16, 512), 0)
        long = pick(jnp.broadcast_to(over_rows(keep(r16 == VECTORS + rank // 8, total)), (8, 512)), (rank % 8) * 64)
        for n in range(VECTORS):
            out_small[n][...] = own[n:n + 1, 0:16]
        out_small[VECTORS][...] = long[0:1, 0:64]
        done = go(SA, 4)
        out_sq[:, 0:1024] = done[0]
        out_sq[:, 1024:1536] = done[1][:, LEFT]
        out_sp[...] = done[1][:, RIGHT]
    else:
        for n in range(VECTORS + 4):
            gvec_out[n:n + 1, :] = gvec[n]
        gvec_out[VECTORS + 4:, :] = jnp.zeros((3, 512), f32)
    for move in out_moves:
        move.wait()


def shards(mesh, *args):
    (tokens, cotangent, sample_count, feature_count, sample_gain, sample_shift, sample_qkv, sample_proj, sample_bias,
     feature_gain, feature_shift, feature_qkv, feature_proj, feature_bias, mlp_gain, mlp_shift, up_weight, up_bias,
     down_weight, down_bias) = args
    T, W = mesh.shape["task"], mesh.shape["wide"]
    micro, _, length, _, width = tokens.shape
    groups = length // W // TILE
    direct = sample_qkv.shape[0] == TILE and T == 4 and W == 8
    axes = ("task", "wide")
    columns = lambda v: v.transpose(0, 1, 3, 2, 4)
    tok = columns(tokens).reshape(micro, length, width)
    cot = columns(cotangent).reshape(micro, W * groups, TILE, width)
    vectors = (sample_gain, sample_shift, sample_bias, feature_gain, feature_shift, feature_bias, mlp_gain, mlp_shift, down_bias)
    V = pl.BlockSpec(memory_space=pltpu.VMEM)
    S = pl.BlockSpec(memory_space=pltpu.SMEM)
    sds = lambda shape, dtype=bf16: jax.ShapeDtypeStruct(shape, dtype)
    dma = lambda *shape: pltpu.SemaphoreType.DMA(shape)
    square, tall = (2, *SPLIT, TILE, 1024), (2, *SPLIT, 64, 256)
    by_sample = (micro, groups, W, TILE, width)
    by_feature = (micro, W * groups, TILE, width)
    saved = [sds(by_sample), sds(by_sample), sds((micro, length, 3 * width)), sds((micro, length, width)), sds((micro, length, 128), f32)]
    params = lambda n: pltpu.CompilerParams(collective_id=n, has_side_effects=True, vmem_limit_bytes=63 * MIB)
    if direct:
        small = jnp.zeros((16, 128), bf16)
        small = jnp.concatenate(
            [jnp.pad(jnp.stack(vectors), ((0, 0), (0, 112))), jnp.pad(up_bias[None], ((0, 6), (0, 64)))], 0
        )
        first_in = (sample_count, tok, cot, sample_qkv, sample_proj, feature_qkv, feature_proj, up_weight, down_weight, small)
        outs = saved + [sds((16, width), f32), sds(square), sds(square), sds(square), sds(tall)]
        scratch = [pltpu.VMEM((SUM_SLOTS, 16, width), bf16), dma(8, 6, 2), dma(6, 2)]
    else:
        gather = lambda v: lax.all_gather(v, axes, axis=0, tiled=True)
        sq, sp, fq, fp, up, dn = map(gather, (sample_qkv, sample_proj, feature_qkv, feature_proj, up_weight, down_weight))
        pair = lambda q, o: jnp.stack([q[:, 0:1024], jnp.concatenate([q[:, 1024:], o], 1)]).reshape(square)
        A, B = pair(sq, sp), pair(fq, fp)
        C = jnp.stack([up[:, 0:1024], up[:, 1024:]]).reshape(square)
        D = jnp.stack([dn[:, 0:256], dn[:, 256:]]).reshape(tall)
        vec = jnp.concatenate([jnp.stack([gather(v) for v in vectors]), gather(up_bias).reshape(4, width), jnp.zeros((3, width), bf16)], 0)
        first_in = (sample_count, tok, cot, A, vec)
        outs, scratch = saved, []
    done = pl.pallas_call(
        lambda *refs: first_kernel(direct, W, groups, *refs), name="samples_forward",
        in_specs=[S] + [V] * (len(first_in) - 1), out_specs=[V] * len(outs), out_shape=outs,
        scratch_shapes=[pltpu.VMEM(by_feature, bf16)] + scratch + [dma(4, W, 2)],
        compiler_params=params(1),
    )(*first_in)
    arr, cots, qkv, o, lse = done[:5]
    if direct:
        vec, A, B, C, D = done[5:]
    second_in = (sample_count, feature_count, tok, arr, cots, qkv, o, lse, vec, A, B, C, D)
    outs = [sds(by_feature), sds((micro, length, width))]
    full = [pltpu.VMEM((length, n * width), kind) for n, kind in
            ((3, bf16), (1, bf16))] + [pltpu.VMEM((length, 128), f32)] + [pltpu.VMEM((length, n * width), kind) for n, kind in
            ((1, f32), (1, f32), (1, bf16), (1, f32))]
    scratch = [pltpu.VMEM(by_sample, bf16), pltpu.VMEM(by_sample, bf16), pltpu.VMEM(by_feature, bf16),
               pltpu.VMEM((16, 1, width), f32), pltpu.VMEM((16, 1, width), f32)] + full
    if direct:
        outs += [sds(v.shape, f32) for v in (sample_qkv, sample_proj, feature_qkv, feature_proj, up_weight, down_weight)]
        outs += [sds((1, v.shape[0]), f32) for v in (*vectors, up_bias)]
        scratch += [pltpu.VMEM(square, f32), pltpu.VMEM(square, f32), pltpu.VMEM(tall, f32),
                    pltpu.VMEM((SUM_SLOTS, 16, width), f32), dma(6, 2), dma(8, 6, 2)]
        for n in range(4):
            for u in (0, 1):
                scratch += scatter_bufs(*((TILE, 1024) if n < 3 else (64, 256)), ORDERS[u])
    else:
        outs += [sds(square, f32)] * 3 + [sds(tall, f32), sds((16, width), f32)]
    done = pl.pallas_call(
        lambda *refs: second_kernel(direct, W, groups, *refs), name="features_and_backward",
        in_specs=[S, S] + [V] * (len(second_in) - 2), out_specs=[V] * len(outs), out_shape=outs,
        scratch_shapes=scratch + [dma(4, W, 2)], compiler_params=params(2),
    )(*second_in)
    restore = lambda v: columns(v.reshape(micro, 1, 1, length, width))
    output, input_grad = restore(done[0]), restore(done[1])
    if direct:
        g_sq, g_sp, g_fq, g_fp, g_up, g_dn = done[2:8]
        g = [v.reshape(-1) for v in done[8:18]]
    else:
        gA, gB, gC, gD, gv = done[2:7]
        two = lambda v: v.reshape(2, -1, v.shape[-1])
        joined = lambda v: jnp.concatenate([two(v)[0], two(v)[1]], 1)
        a, b = joined(gA), joined(gB)
        scatter = lambda v: lax.psum_scatter(v, axes, scatter_dimension=0, tiled=True)
        g_sq, g_sp, g_fq, g_fp, g_up, g_dn = map(scatter, (a[:, :1536], a[:, 1536:], b[:, :1536], b[:, 1536:], joined(gC), joined(gD)))
        g = [scatter(gv[n]) for n in range(VECTORS)] + [scatter(gv[VECTORS:VECTORS + 4].reshape(-1))]
    return (output, input_grad, g[0], g[1], g_sq, g_sp, g[2], g[3], g[4], g_fq, g_fp, g[5], g[6], g[7], g_up, g[9], g_dn, g[8])


def solution(mesh):
    rows = P(("task", "wide"))
    table = P(("task", "wide"), None)
    data = P(None, "task", None, "wide", None)
    params = (rows, rows, table, table, rows, rows, rows, table, table, rows, rows, rows, table, rows, table, rows)
    counts = P(None, "task")

    def run(*args):
        return shards(mesh, *args)

    return jax.shard_map(
        run, mesh=mesh, in_specs=(data, data, counts, counts) + params, out_specs=(data, data) + params, check_vma=False
    )
```

```python
import jax
import jax.numpy as jnp
from jax import lax
from jax.experimental import pallas as pl
from jax.experimental.pallas import tpu as pltpu
from jax.sharding import PartitionSpec as P

HEADS = 8
HEAD_SIZE = 64
PAIRS = HEADS // 2
SCALE = HEAD_SIZE ** -0.5
TILE = 16
SPLIT = (2, 2, 4, 2)

epsilon = 1e-05
masked_score = -1e30
f32, bf16 = jnp.float32, jnp.bfloat16
MESH = pl.DeviceIdType.MESH
MIB = 1 << 20


def mm(a, b):
    return lax.dot_general(a, b, (((1,), (0,)), ((), ())), preferred_element_type=f32)


def mm_nt(a, b):
    return lax.dot_general(a, b, (((1,), (1,)), ((), ())), preferred_element_type=f32)


def mm_tn(a, b):
    return lax.dot_general(a, b, (((0,), (0,)), ((), ())), preferred_element_type=f32)


def flat(value):
    return value.reshape(-1, value.shape[-1])


def normed(v):
    centred = v - jnp.mean(v, -1, keepdims=True)
    scale = lax.rsqrt(jnp.mean(centred * centred, -1, keepdims=True) + epsilon)
    return centred * scale, scale


def normed_back(grad, unit, scale, gain):
    t = grad * gain
    return scale * (t - jnp.mean(t, -1, keepdims=True) - unit * jnp.mean(t * unit, -1, keepdims=True))


def over_rows(v):
    return jnp.sum(v, 0, keepdims=True)


def gelu_parts(x):
    t = 1.0 / (1.0 + 0.3275911 * 0.5 ** 0.5 * jnp.abs(x))
    e = jnp.exp(-0.5 * (x * x))
    poly = t * (0.127414796 + t * (-0.142248368 + t * (0.7107068705 + t * (-0.7265760135 + t * 0.5307027145))))
    tail = poly * e
    return jnp.where(x >= 0, 1.0 - tail, tail), e


def half_mask(half):
    lane = lax.broadcasted_iota(jnp.int32, (1, 128), 1)
    return (lane < HEAD_SIZE) if half == 0 else (lane >= HEAD_SIZE)


def keep(mask, v):
    return jnp.where(mask, v, jnp.zeros_like(v))


def lanes(part, j):
    start = part * 512 + j * 128
    return pl.ds(start if isinstance(j, int) else pl.multiple_of(start, 128), 128)


def mask_lanes(rows, keys, group):
    lane = lax.broadcasted_iota(jnp.int32, (rows, 128), 1) % HEAD_SIZE
    row = lax.broadcasted_iota(jnp.int32, (rows, 128), 0)
    ones = (lane == row % group).astype(bf16)
    off = (lane < group) & ((lane != row % group) | (row // group >= keys))
    return ones, jnp.where(off, masked_score, 0.0).astype(bf16)


def slot(ref, base, n, size):
    side = 512 // size
    if side == 1:
        return ref.at[base + n]
    n, row, col = n // (side * side), n // side % side, n % side
    return ref.at[base + n, row * size:(row + 1) * size, col * size:(col + 1) * size]


def attend(jobs, size, extra, qkv, o, lse, wide, narrow):
    ones, off = extra
    for i, (rows, j, at) in enumerate(jobs):
        q = qkv[rows, lanes(0, j)] * jnp.asarray(SCALE, bf16)
        k = qkv[rows, lanes(1, j)]
        for half in (0, 1):
            msk = half_mask(half)
            slot(wide, 0, 2 * i + half, size)[...] = mm_nt(jnp.where(msk, k, off), jnp.where(msk, q, ones))
    for i, (rows, j, at) in enumerate(jobs):
        for half in (0, 1):
            s = slot(wide, 0, 2 * i + half, size)[...]
            top = jnp.max(s, 0, keepdims=True)
            e = jnp.exp(s - top)
            mass = over_rows(e)
            slot(narrow, 0, 2 * i + half, size)[...] = (e * (1.0 / mass)).astype(bf16)
            lse[at(2 * j + half)] = top + jnp.log(mass)
    for i, (rows, j, at) in enumerate(jobs):
        v = qkv[rows, lanes(2, j)]
        a, b = (mm_tn(slot(narrow, 0, 2 * i + half, size)[...], v) for half in (0, 1))
        o[rows, lanes(0, j)] = jnp.where(half_mask(0), a, b).astype(bf16)


def attend_back(jobs, size, extra, qkv, o, lse, do, dqkv, wide, narrow):
    ones, off = extra
    head = lax.broadcasted_iota(jnp.int32, (8, 128), 1) // HEAD_SIZE
    pick = (head == lax.broadcasted_iota(jnp.int32, (8, 128), 0)).astype(bf16)
    deltas = []
    for i, (rows, j, at) in enumerate(jobs):
        q = qkv[rows, lanes(0, j)] * jnp.asarray(SCALE, bf16)
        k = qkv[rows, lanes(1, j)]
        v = qkv[rows, lanes(2, j)]
        d = do[rows, lanes(0, j)]
        prod = d.astype(f32) * o[rows, lanes(0, j)].astype(f32)
        high = prod.astype(bf16)
        deltas.append(mm_nt(pick, high) + mm_nt(pick, (prod - high.astype(f32)).astype(bf16)))
        for half in (0, 1):
            msk = half_mask(half)
            slot(wide, 0, 2 * i + half, size)[...] = mm_nt(jnp.where(msk, k, off), jnp.where(msk, q, ones))
            slot(wide, 2, 2 * i + half, size)[...] = mm_nt(v, keep(msk, d))
    for i, (rows, j, at) in enumerate(jobs):
        for half in (0, 1):
            p = jnp.exp(slot(wide, 0, 2 * i + half, size)[...] - lse[at(2 * j + half)])
            slot(narrow, 0, 2 * i + half, size)[...] = p.astype(bf16)
            ds = p * (slot(wide, 2, 2 * i + half, size)[...] - deltas[i][half:half + 1])
            slot(narrow, 2, 2 * i + half, size)[...] = ds.astype(bf16)
    first = half_mask(0)
    for i, (rows, j, at) in enumerate(jobs):
        q = qkv[rows, lanes(0, j)] * jnp.asarray(SCALE, bf16)
        k = qkv[rows, lanes(1, j)]
        d = do[rows, lanes(0, j)]
        p = [slot(narrow, 0, 2 * i + half, size) for half in (0, 1)]
        ds = [slot(narrow, 2, 2 * i + half, size) for half in (0, 1)]
        dq = jnp.where(first, mm_tn(ds[0][...], k), mm_tn(ds[1][...], k)) * SCALE
        dk = jnp.where(first, mm(ds[0][...], q), mm(ds[1][...], q))
        dv = jnp.where(first, mm(p[0][...], d), mm(p[1][...], d))
        dqkv[rows, lanes(0, j)] = dq.astype(bf16)
        dqkv[rows, lanes(1, j)] = dk.astype(bf16)
        dqkv[rows, lanes(2, j)] = dv.astype(bf16)


def loop(n, body, unrolled=False):
    if unrolled:
        for i in range(n):
            body(i)
    else:
        def step(i, carry):
            body(i)
            return carry
        lax.fori_loop(0, n, step, 0)


def project(h, W, qkv):
    qkv[:, 0:1024] = mm(h, flat(W[0])).astype(bf16)
    qkv[:, 1024:1536] = mm(h, flat(W[1, ..., 0:512])).astype(bf16)


def out_proj(W):
    return flat(W[1, ..., 512:1024])


def put(ref, index, value, add):
    value = value.reshape(ref.at[index].shape)
    if add is False:
        ref[index] = value
    else:
        ref[index] = ref[index] + value


LEFT, RIGHT = slice(0, 512), slice(512, 1024)


class Place:
    def __init__(self, W):
        self.t, self.w, self.W = lax.axis_index("task"), lax.axis_index("wide"), W
        self.x, self.c = self.t // 2, self.t % 2
        self.z, self.y = self.w // 2, self.w % 2

    def barrier(self, direct):
        peers = [(self.t, (self.w + i) % self.W) for i in range(1, self.W)]
        if direct:
            peers += [(self.t + 1 - 2 * self.c, self.w), ((self.t + 2) % 4, self.w)]
        bar = pltpu.get_barrier_semaphore()
        for peer in peers:
            pl.semaphore_signal(bar, inc=1, device_id=peer, device_id_type=MESH)
        pl.semaphore_wait(bar, len(peers))

    def other(self, axis):
        if axis == "c":
            return (self.t + 1 - 2 * self.c, self.w)
        if axis == "x":
            return ((self.t + 2) % 4, self.w)
        return (self.t, self.w + 1 - 2 * self.y)

    def along_z(self, step):
        return (self.t, (self.w + 2 * step) % 8)


def remote(src, dst, sems, device):
    return pltpu.make_async_remote_copy(
        src_ref=src, dst_ref=dst, send_sem=sems.at[0], recv_sem=sems.at[1], device_id=device, device_id_type=MESH
    )


class Exchange:
    def __init__(self, place, src, dst, sems):
        me, W = place.w, place.W
        self.copies = []
        for i in range(W - 1, 0, -1):
            peer = (me + i) % W
            self.copies.append(remote(src(peer), dst(me), sems.at[i], (place.t, peer)))
        self.copies.append(pltpu.make_async_copy(src(me), dst(me), sems.at[0, 0]))

    def start(self):
        for copy in self.copies:
            copy.start()

    def wait(self):
        for copy in self.copies:
            copy.wait()


class Gather:
    def __init__(self, place, ref, order, sems):
        x, c, z, y = place.x, place.c, place.z, place.y
        own = ref.at[x, c, z, y]
        self.stages = [[remote(own, own, sems.at[s - 1], place.along_z(s)) for s in (1, 2, 3)]]
        line = ref.at[x, c, :, y]
        if order == "yx":
            plane = ref.at[x, c]
            self.stages.append([remote(line, line, sems.at[3], place.other("y"))])
            self.stages.append([remote(plane, plane, sems.at[4], place.other("x"))])
        else:
            plane = ref.at[:, c, :, y]
            self.stages.append([remote(line, line, sems.at[3], place.other("x"))])
            self.stages.append([remote(plane, plane, sems.at[4], place.other("y"))])
        half = ref.at[:, c]
        self.stages.append([remote(half, half, sems.at[5], place.other("c"))])

    def start(self, stage):
        for copy in self.stages[stage]:
            copy.start()

    def wait(self, stage):
        for copy in self.stages[stage]:
            copy.wait()


class SumAll:
    def __init__(self, place, slots, sems):
        peers = [[place.along_z(s) for s in (1, 2, 3)], [place.other("y")], [place.other("x")], [place.other("c")]]
        self.slots, self.stages, n = slots, [], 0
        for group in peers:
            stage = []
            for peer in group:
                stage.append((n, peer))
                n += 1
            self.stages.append(stage)
        self.copies = [
            [remote(slots.at[s], slots.at[4 + n], sems.at[n], peer) for n, peer in stage]
            for s, stage in enumerate(self.stages)
        ]

    def start(self, stage, value=None):
        if stage == 0:
            self.slots[0] = value
        for copy in self.copies[stage]:
            copy.start()

    def wait(self, stage):
        total = self.slots[stage].astype(f32)
        for copy, (n, _) in zip(self.copies[stage], self.stages[stage]):
            copy.wait()
            total = total + self.slots[4 + n].astype(f32)
        if stage < 3:
            self.slots[stage + 1] = total.astype(self.slots.dtype)
        return total


SUM_SLOTS = 10


class Scatter:
    def __init__(self, place, grad, order, bufs, sems):
        self.p, self.grad, self.order, self.sems = place, grad, order, sems
        self.recv, self.s1, self.r1, self.r2, self.r3 = bufs
        self.s2 = self.s3 = self.s1.at[:, 0] if order == "xy" else self.s1.at[0]
        x, c, z, y = place.x, place.c, place.z, place.y
        self.core = remote(grad.at[:, 1 - c], self.recv, sems.at[0], place.other("c"))
        first, second = ("x", "y") if order == "xy" else ("y", "x")
        self.one = remote(self.s1, self.r1, sems.at[1], place.other(first))
        self.two = remote(self.s2, self.r2, sems.at[2], place.other(second))
        self.three = [
            remote(self.s3.at[(z + s) % 4], self.r3.at[s - 1], sems.at[2 + s], place.along_z(s)) for s in (1, 2, 3)
        ]

    def step(self, stage):
        x, c, z, y = self.p.x, self.p.c, self.p.z, self.p.y
        xy = self.order == "xy"
        sums = self.recv
        if stage == 0:
            self.core.start()
        elif stage == 1:
            self.core.wait()
            sums[...] = sums[...] + self.grad[:, c]
            self.s1[...] = (sums[1 - x] if xy else sums[:, :, 1 - y]).astype(bf16)
            self.one.start()
        elif stage == 2:
            self.one.wait()
            if xy:
                sums[x] = sums[x] + self.r1[...].astype(f32)
                self.s2[...] = sums[x, :, 1 - y].astype(bf16)
            else:
                sums[:, :, y] = sums[:, :, y] + self.r1[...].astype(f32)
                self.s2[...] = sums[1 - x, :, y].astype(bf16)
            self.two.start()
        elif stage == 3:
            self.two.wait()
            sums[x, :, y] = sums[x, :, y] + self.r2[...].astype(f32)
            self.s3[...] = sums[x, :, y].astype(bf16)
            for copy in self.three:
                copy.start()
        else:
            total = sums[x, z, y]
            for i, copy in enumerate(self.three):
                copy.wait()
                total = total + self.r3[i].astype(f32)
            return total


def scatter_bufs(rows, cols, order):
    first = (4, 2, rows, cols) if order == "xy" else (2, 4, rows, cols)
    return [
        pltpu.VMEM((2, 4, 2, rows, cols), f32),
        pltpu.VMEM(first, bf16), pltpu.VMEM(first, bf16),
        pltpu.VMEM((4, rows, cols), bf16), pltpu.VMEM((3, rows, cols), bf16),
    ]


ORDERS = ("yx", "xy")


VECTORS = 9


def layer_kernel(direct, W, groups, *refs):
    refs = list(refs)
    take = lambda n: [refs.pop(0) for _ in range(n)]
    count_s, count_f, tok, cot = take(4)
    if direct:
        sq, sp, fq, fp, up, dn, small = take(7)
    else:
        A, B, C, D, vec_in = take(5)
    result, gin = take(2)
    if direct:
        out_sq, out_sp, out_fq, out_fp, out_up, out_dn = take(6)
        out_small = take(10)
    else:
        gA, gB, gC, gD, gvec_out = take(5)
    arr, cots, leave, gleave, grecv, qkv_s, o_s, lse_s = take(8)
    vec, gvec, qkv, o, lse, stream, h2, wide, narrow = take(9)
    dqkv, do = qkv, h2
    dout, dh2 = wide.at[2], wide.at[3]
    if direct:
        A, B, C, D, gB, gC, gD = take(7)
        gA = gC
        vslots, gslots, wsems, vsems, gsems, ssems = take(6)
        bufs = [take(5) for _ in range(8)]
    xsems, lsems = take(2)
    p = Place(W)
    t, w = p.t, p.w
    rank = t * 8 + w
    block_rows = W * TILE

    def of_peer(ref, m):
        return lambda peer: ref.at[m, peer * groups // W, pl.ds(peer * groups % W, groups)]

    of_cot = lambda m: lambda peer: cot.at[m, pl.ds(peer * groups, groups)]
    by_feature = lambda ref, m: lambda peer: ref.at[m, :, peer]
    by_sample = lambda ref, m: lambda peer: ref.at[m, pl.ds(peer * groups, groups)]
    cot_moves = [Exchange(p, of_cot(m), by_feature(cots, m), xsems.at[m]) for m in (0, 1)]
    first_moves = [Exchange(p, of_peer(leave, m), by_feature(arr, m), xsems.at[2 + m]) for m in (0, 1)]
    out_moves = [Exchange(p, by_feature(leave, m), by_sample(result, m), xsems.at[4 + m]) for m in (0, 1)]
    back_moves = [Exchange(p, by_feature(gleave, m), by_sample(grecv, m), xsems.at[6 + m]) for m in (0, 1)]
    gin_moves = [pltpu.make_async_copy(grecv.at[m], gin.at[m], lsems.at[m]) for m in (0, 1)]
    GA = GB = GC = GD = SA = SB = SC = SD = ()
    if direct:
        gathers = [Gather(p, ref.at[u], ORDERS[u], wsems.at[2 * n + u]) for n, ref in enumerate((A, B, C, D)) for u in (0, 1)]
        GA, GB, GC, GD = gathers[0:2], gathers[2:4], gathers[4:6], gathers[6:8]
        scatters = [
            Scatter(p, ref.at[u], ORDERS[u], bufs[2 * n + u], ssems.at[2 * n + u])
            for n, ref in enumerate((gA, gB, gC, gD)) for u in (0, 1)
        ]
        SA, SB, SC, SD = scatters[0:2], scatters[2:4], scatters[4:6], scatters[6:8]

    def pull(group, stage):
        for g in group:
            if stage > 0:
                g.wait(stage - 1)
            if stage < 4:
                g.start(stage)

    def push(group, stage):
        return [s.step(stage) for s in group]

    p.barrier(direct)
    if direct:
        at = (p.x, p.c, p.z, p.y)
        A[(0, *at)] = sq[:, 0:1024]
        A[(1, *at, slice(None), LEFT)] = sq[:, 1024:1536]
        A[(1, *at, slice(None), RIGHT)] = sp[...]
        pull(GA, 0)
        n, l = (lax.broadcasted_iota(jnp.int32, (16, 256), d) for d in (0, 1))
        short = (l < VECTORS * 16) & (l // 16 == n)
        long = (l >= VECTORS * 16) & (l < VECTORS * 16 + 64) & (n == VECTORS + rank // 8)
        spread = jnp.where(short | long, jnp.broadcast_to(small[...], (16, 256)), jnp.zeros((16, 256), bf16))
        l, j = (lax.broadcasted_iota(jnp.int32, (256, 512), d) for d in (0, 1))
        goal = jnp.where(l < VECTORS * 16, rank * 16 + l % 16, rank % 8 * 64 + l - VECTORS * 16)
        both = SumAll(p, vslots, vsems)
        both.start(0, mm(spread, (j == goal).astype(bf16)).astype(bf16))
        B[(0, *at)] = fq[:, 0:1024]
        B[(1, *at, slice(None), LEFT)] = fq[:, 1024:1536]
        B[(1, *at, slice(None), RIGHT)] = fp[...]
        for u in (0, 1):
            C[(u, *at)] = up[:, 1024 * u:1024 * u + 1024]
            D[(u, *at)] = dn[:, 256 * u:256 * u + 256]
        both.wait(0)
        both.start(1)
        pull(GA, 1)
        cot_moves[0].start()
        both.wait(1)
        both.start(2)
        pull(GB, 0)
        pull(GA, 2)
        both.wait(2)
        both.start(3)
        pull(GC, 0)
        pull(GB, 1)
        pull(GA, 3)
        rows = both.wait(3)
        for n in range(16):
            vec[n] = rows[n:n + 1]
        pull(GA, 4)
    else:
        cot_moves[0].start()
        for n in range(16):
            vec[n] = vec_in[n:n + 1, :].astype(f32)
    row = lambda n: vec[n]
    everything = slice(None)

    def sample_pairs(body):
        loop(PAIRS, lambda n: body([(everything, n, lambda h: h)], 512))

    def samples(m):
        extra = mask_lanes(512, count_s[0, m], 1)
        unit, _ = normed(tok[m].astype(f32))
        project((unit * row(0) + row(1)).astype(bf16), A, qkv_s.at[m])
        if m == 0:
            pull(GB, 2)
            pull(GC, 1)
            pull(GD, 0)
        else:
            pull(GB, 4)
            pull(GC, 3)
            pull(GD, 2)
        sample_pairs(lambda jobs, size: attend(jobs, size, extra, qkv_s.at[m], o_s.at[m], lse_s.at[m], wide, narrow))
        if m == 0:
            pull(GC, 2)
            pull(GD, 1)
            pull(GB, 3)
        else:
            pull(GC, 4)
            pull(GD, 3)
        branch = mm(o_s[m], out_proj(A)) + row(2)
        leave[m] = (tok[m].astype(f32) + branch).astype(bf16).reshape(leave.shape[1:])
        first_moves[m].start()

    def features(m):
        add = m > 0
        extra = mask_lanes(block_rows, count_f[0, m], TILE)

        def blocks(body):
            def jobs_of(g, pairs):
                rows = pl.ds(g * block_rows, block_rows)
                return [(rows, n, lambda h: (h, everything, rows)) for n in pairs]

            if block_rows == 128:
                body([job for g in range(groups) for job in jobs_of(g, range(PAIRS))], block_rows)
            else:
                for g in range(groups):
                    loop(PAIRS, lambda n: body(jobs_of(g, [n]), block_rows))

        first_moves[m].wait()
        x = flat(arr[m]).astype(f32)
        unit, _ = normed(x)
        project((unit * row(3) + row(4)).astype(bf16), B, qkv)
        blocks(lambda jobs, size: attend(jobs, size, extra, qkv, o, lse, wide, narrow))
        s2 = flat(arr[m]).astype(f32) + mm(o[...], out_proj(B)) + row(5)
        stream[...] = s2
        unit, _ = normed(s2)
        h2[...] = (unit * row(6) + row(7)).astype(bf16)
        if m == 0:
            pull(GD, 4)
        cot_moves[m].wait()
        if m == 0:
            cot_moves[1].start()

        def chunk(n):
            half = n // 2
            cols = pl.ds(pl.multiple_of((n % 2) * 512, 512), 512)
            upw = C[half, :, :, :, :, :, cols].reshape(512, 512)
            d0 = D[0, n // 2, n % 2].reshape(512, 256)
            d1 = D[1, n // 2, n % 2].reshape(512, 256)
            g16 = flat(cots[m])
            wide[0] = mm(h2[...], upw) + vec[VECTORS + n]
            wide[1] = mm_nt(g16[:, 0:256], d0) + mm_nt(g16[:, 256:512], d1)
            total = jnp.zeros((8, 512), f32)
            for r in range(0, 512, 64):
                part = slice(r, r + 64)
                raised = wide[0, part]
                phi, e = gelu_parts(raised)
                narrow[0, part] = (raised * phi).astype(bf16)
                draised = (wide[1, part] * (phi + raised * e * (0.5 / jnp.pi) ** 0.5)).astype(bf16)
                narrow[1, part] = draised
                total = total + jnp.sum(draised.astype(f32).reshape(8, 8, 512), 0)
            put(gvec, VECTORS + n, over_rows(total), add)
            a0, a1, b0 = mm(narrow[0], d0), mm(narrow[0], d1), mm_nt(narrow[1], upw)

            @pl.when(n == 0)
            def _():
                dout[:, 0:256] = a0
                dout[:, 256:512] = a1
                dh2[...] = b0

            @pl.when(n > 0)
            def _():
                dout[:, 0:256] += a0
                dout[:, 256:512] += a1
                dh2[...] += b0

            put(gC, (half, *[everything] * 5, cols), mm_tn(h2[...], narrow[1]), add)
            put(gD, (0, n // 2, n % 2), mm_tn(narrow[0], g16[:, 0:256]), add)
            put(gD, (1, n // 2, n % 2), mm_tn(narrow[0], g16[:, 256:512]), add)

        loop(4, chunk)
        leave[m] = (stream[...] + dout[...] + row(8)).astype(bf16).reshape(leave.shape[1:])
        out_moves[m].start()
        if m == 1:
            push(SC, 0)
            push(SD, 0)
        cot16 = flat(cots[m]).astype(f32)
        put(gvec, 8, over_rows(cot16), add)
        unit, scale = normed(stream[...])
        dh = dh2[...]
        put(gvec, 6, over_rows(dh * unit), add)
        put(gvec, 7, over_rows(dh), add)
        g2 = cot16 + normed_back(dh, unit, scale, row(6))
        stream[...] = g2
        gy = g2.astype(bf16)
        put(gB, (1, Ellipsis, RIGHT), mm_tn(o[...], gy), add)
        put(gvec, 5, over_rows(gy.astype(f32)), add)
        do[...] = mm_nt(gy, out_proj(B)).astype(bf16)
        blocks(lambda jobs, size: attend_back(jobs, size, extra, qkv, o, lse, do, dqkv, wide, narrow))
        if m == 1:
            push(SC, 1)
            push(SD, 1)
        unit, scale = normed(flat(arr[m]).astype(f32))
        h = (unit * row(3) + row(4)).astype(bf16)
        dh = mm_nt(dqkv[:, 0:1024], flat(B[0])) + mm_nt(dqkv[:, 1024:1536], flat(B[1, ..., LEFT]))
        gleave[m] = (stream[...] + normed_back(dh, unit, scale, row(3))).astype(bf16).reshape(gleave.shape[1:])
        back_moves[m].start()
        put(gvec, 3, over_rows(dh * unit), add)
        put(gvec, 4, over_rows(dh), add)
        put(gB, 0, mm_tn(h, dqkv[:, 0:1024]), add)
        put(gB, (1, Ellipsis, LEFT), mm_tn(h, dqkv[:, 1024:1536]), add)

    def samples_back(m, service):
        add = m > 0
        extra = mask_lanes(512, count_s[0, m], 1)
        back_moves[m].wait()
        gy = flat(grecv[m])
        put(gA, (1, Ellipsis, RIGHT), mm_tn(o_s[m], gy), add)
        put(gvec, 2, over_rows(gy.astype(f32)), add)
        do[...] = mm_nt(gy, out_proj(A)).astype(bf16)
        service(0)
        sample_pairs(
            lambda jobs, size: attend_back(jobs, size, extra, qkv_s.at[m], o_s.at[m], lse_s.at[m], do, dqkv, wide, narrow)
        )
        service(1)
        unit, scale = normed(tok[m].astype(f32))
        h = (unit * row(0) + row(1)).astype(bf16)
        put(gA, 0, mm_tn(h, dqkv[:, 0:1024]), add)
        put(gA, (1, Ellipsis, LEFT), mm_tn(h, dqkv[:, 1024:1536]), add)
        if m == 1:
            push(SA, 0)
        dh = mm_nt(dqkv[:, 0:1024], flat(A[0])) + mm_nt(dqkv[:, 1024:1536], flat(A[1, ..., LEFT]))
        put(gvec, 0, over_rows(dh * unit), add)
        put(gvec, 1, over_rows(dh), add)
        grecv[m] = (flat(grecv[m]).astype(f32) + normed_back(dh, unit, scale, row(0))).astype(bf16).reshape(grecv.shape[1:])
        gin_moves[m].start()

    samples(0)
    samples(1)
    features(0)
    features(1)
    push(SB, 0)

    def service0(k):
        if k == 0:
            push(SC, 2)
            push(SD, 2)
            push(SB, 1)
        else:
            push(SC, 3)
            push(SD, 3)
            push(SB, 2)

    def service1(k):
        if k == 0:
            done = push(SC, 4) + push(SD, 4)
            if direct:
                out_up[:, 0:1024], out_up[:, 1024:2048], out_dn[:, 0:256], out_dn[:, 256:512] = done
            push(SB, 3)
        elif direct:
            done = push(SB, 4)
            out_fq[:, 0:1024] = done[0]
            out_fq[:, 1024:1536] = done[1][:, LEFT]
            out_fp[...] = done[1][:, RIGHT]

    samples_back(0, service0)
    samples_back(1, service1)
    if direct:
        both = SumAll(p, gslots, gsems)
        both.start(0, jnp.concatenate([gvec[n] for n in range(VECTORS + 4)] + [jnp.zeros((3, 512), f32)], 0))
        push(SA, 1)
        both.wait(0)
        both.start(1)
        push(SA, 2)
        both.wait(1)
        both.start(2)
        push(SA, 3)
        both.wait(2)
        both.start(3)
        total = both.wait(3)
        l, j = (lax.broadcasted_iota(jnp.int32, (512, 128), d) for d in (0, 1))
        pick = lambda v, start: lax.dot_general(
            v, (l == start + j).astype(f32), (((1,), (0,)), ((), ())), precision=lax.Precision.HIGHEST, preferred_element_type=f32
        )
        own = pick(total, rank * 16)
        n = lax.broadcasted_iota(jnp.int32, (16, 512), 0)
        long = pick(jnp.broadcast_to(over_rows(keep(n == VECTORS + rank // 8, total)), (8, 512)), rank % 8 * 64)
        for n in range(VECTORS):
            out_small[n][...] = own[n:n + 1, 0:16]
        out_small[VECTORS][...] = long[0:1, 0:64]
        done = push(SA, 4)
        out_sq[:, 0:1024] = done[0]
        out_sq[:, 1024:1536] = done[1][:, LEFT]
        out_sp[...] = done[1][:, RIGHT]
    else:
        for n in range(VECTORS + 4):
            gvec_out[n:n + 1, :] = gvec[n]
        gvec_out[VECTORS + 4:, :] = jnp.zeros((3, 512), f32)
    for move in out_moves + gin_moves:
        move.wait()


def copy_kernel(*refs):
    n = len(refs) // 2
    for source, goal in zip(refs[:n], refs[n:]):
        goal[...] = source[...]


def shards(mesh, *args):
    (tokens, cotangent, sample_count, feature_count, sample_gain, sample_shift, sample_qkv, sample_proj, sample_bias,
     feature_gain, feature_shift, feature_qkv, feature_proj, feature_bias, mlp_gain, mlp_shift, up_weight, up_bias,
     down_weight, down_bias) = args
    T, W = mesh.shape["task"], mesh.shape["wide"]
    micro, _, length, _, width = tokens.shape
    groups = length // W // TILE
    direct = sample_qkv.shape[0] == TILE and T == 4 and W == 8
    axes = ("task", "wide")
    by_sample = (micro, groups, W, TILE, width)
    by_feature = (micro, W * groups, TILE, width)
    columns = lambda v: v.transpose(0, 1, 3, 2, 4)
    tok = columns(tokens).reshape(micro, length, width)
    cot = columns(cotangent).reshape(by_feature)
    vectors = (sample_gain, sample_shift, sample_bias, feature_gain, feature_shift, feature_bias, mlp_gain, mlp_shift, down_bias)
    V = pl.BlockSpec(memory_space=pltpu.VMEM)
    S = pl.BlockSpec(memory_space=pltpu.SMEM)
    H = pl.BlockSpec(memory_space=pl.ANY)
    sds = lambda shape, dtype=bf16: jax.ShapeDtypeStruct(shape, dtype)
    dma = lambda *shape: pltpu.SemaphoreType.DMA(shape)
    flat_of = lambda n, kind: pltpu.VMEM((length, n * width), kind)
    logs = pltpu.VMEM((HEADS, 1, length), f32)
    square, tall = (2, *SPLIT, TILE, 1024), (2, *SPLIT, 64, 256)
    scratch = [pltpu.VMEM(by_sample, bf16)] * 4 + [
        pltpu.VMEM(by_feature, bf16), pltpu.VMEM((micro, length, 3 * width), bf16), pltpu.VMEM((micro, length, width), bf16),
        pltpu.VMEM((micro, HEADS, 1, length), f32), pltpu.VMEM((16, 1, width), f32), pltpu.VMEM((16, 1, width), f32),
        flat_of(3, bf16), flat_of(1, bf16), logs, flat_of(1, f32), flat_of(1, bf16),
        pltpu.VMEM((4, length, width), f32), pltpu.VMEM((4, length, width), bf16),
    ]
    matrices = (sample_qkv, sample_proj, feature_qkv, feature_proj, up_weight, down_weight)
    outs = [sds(by_feature), sds(by_feature)]
    counts = (sample_count.T, feature_count.T)
    if direct:
        small = jnp.concatenate([*vectors, up_bias, jnp.zeros(48, bf16)]).reshape(1, 256)
        ins = (*matrices, small)
        outs += [sds(v.shape, f32) for v in matrices] + [sds((1, v.shape[0]), f32) for v in (*vectors, up_bias)]
        scratch += [pltpu.VMEM(square, bf16)] * 3 + [pltpu.VMEM(tall, bf16)] + [pltpu.VMEM(square, f32)] * 2 + [pltpu.VMEM(tall, f32)]
        scratch += [pltpu.VMEM((SUM_SLOTS, 16, width), bf16), pltpu.VMEM((SUM_SLOTS, 16, width), f32)]
        scratch += [dma(8, 6, 2), dma(6, 2), dma(6, 2), dma(8, 6, 2)]
        for n in range(4):
            for u in (0, 1):
                scratch += scatter_bufs(*((TILE, 1024) if n < 3 else (64, 256)), ORDERS[u])
    else:
        gather = lambda v: lax.all_gather(v, axes, axis=0, tiled=True)
        sq, sp, fq, fp, up, dn = map(gather, matrices)
        pair = lambda q, o: jnp.stack([q[:, 0:1024], jnp.concatenate([q[:, 1024:], o], 1)]).reshape(square)
        C = jnp.stack([up[:, 0:1024], up[:, 1024:]]).reshape(square)
        D = jnp.stack([dn[:, 0:256], dn[:, 256:]]).reshape(tall)
        rest = [gather(up_bias).reshape(4, width), jnp.zeros((3, width), bf16)]
        ins = (pair(sq, sp), pair(fq, fp), C, D, jnp.concatenate([jnp.stack([gather(v) for v in vectors]), *rest], 0))
        outs += [sds(square, f32)] * 3 + [sds(tall, f32), sds((16, width), f32)]
    done = pl.pallas_call(
        lambda *refs: layer_kernel(direct, W, groups, *refs), name="layer",
        in_specs=[S, S, V, H] + [V] * len(ins), out_specs=[H, H] + [V] * (len(outs) - 2), out_shape=outs,
        scratch_shapes=scratch + [dma(8, W, 2), dma(2)],
        compiler_params=pltpu.CompilerParams(collective_id=1, has_side_effects=True, vmem_limit_bytes=63 * MIB),
    )(*counts, tok, cot, *ins)
    if direct:
        done = pl.pallas_call(
            copy_kernel, name="hand_out", in_specs=[V] * len(outs), out_specs=[V] * len(outs), out_shape=outs,
        )(*done)
    restore = lambda v: columns(v.reshape(micro, 1, 1, length, width))
    output, input_grad = restore(done[0]), restore(done[1])
    if direct:
        g_sq, g_sp, g_fq, g_fp, g_up, g_dn = done[2:8]
        g = [v.reshape(-1) for v in done[8:18]]
    else:
        gA, gB, gC, gD, gv = done[2:7]
        two = lambda v: v.reshape(2, -1, v.shape[-1])
        joined = lambda v: jnp.concatenate([two(v)[0], two(v)[1]], 1)
        a, b = joined(gA), joined(gB)
        scatter = lambda v: lax.psum_scatter(v, axes, scatter_dimension=0, tiled=True)
        g_sq, g_sp, g_fq, g_fp, g_up, g_dn = map(scatter, (a[:, :1536], a[:, 1536:], b[:, :1536], b[:, 1536:], joined(gC), joined(gD)))
        g = [scatter(gv[n]) for n in range(VECTORS)] + [scatter(gv[VECTORS:VECTORS + 4].reshape(-1))]
    return (output, input_grad, g[0], g[1], g_sq, g_sp, g[2], g[3], g[4], g_fq, g_fp, g[5], g[6], g[7], g_up, g[9], g_dn, g[8])


def solution(mesh):
    rows = P(("task", "wide"))
    table = P(("task", "wide"), None)
    data = P(None, "task", None, "wide", None)
    params = (rows, rows, table, table, rows, rows, rows, table, table, rows, rows, rows, table, rows, table, rows)
    counts = P(None, "task")

    def run(*args):
        return shards(mesh, *args)

    return jax.shard_map(
        run, mesh=mesh, in_specs=(data, data, counts, counts) + params, out_specs=(data, data) + params, check_vma=False
    )
```

```python
import jax
import jax.numpy as jnp
from jax import lax
from jax.experimental import pallas as pl
from jax.experimental.pallas import tpu as pltpu
from jax.sharding import PartitionSpec as P

HEADS = 8
HEAD_SIZE = 64
PAIRS = HEADS // 2
SCALE = HEAD_SIZE ** -0.5
TILE = 16
SPLIT = (2, 2, 4, 2)

epsilon = 1e-05
masked_score = -1e30
f32, bf16 = jnp.float32, jnp.bfloat16
MESH = pl.DeviceIdType.MESH
MIB = 1 << 20


def mm(a, b):
    return lax.dot_general(a, b, (((1,), (0,)), ((), ())), preferred_element_type=f32)


def mm_nt(a, b):
    return lax.dot_general(a, b, (((1,), (1,)), ((), ())), preferred_element_type=f32)


def mm_tn(a, b):
    return lax.dot_general(a, b, (((0,), (0,)), ((), ())), preferred_element_type=f32)


def flat(value):
    return value.reshape(-1, value.shape[-1])


def normed(v):
    centred = v - jnp.mean(v, -1, keepdims=True)
    scale = lax.rsqrt(jnp.mean(centred * centred, -1, keepdims=True) + epsilon)
    return centred * scale, scale


def normed_back(grad, unit, scale, gain):
    t = grad * gain
    return scale * (t - jnp.mean(t, -1, keepdims=True) - unit * jnp.mean(t * unit, -1, keepdims=True))


def over_rows(v):
    return jnp.sum(v, 0, keepdims=True)


def gelu_parts(x):
    t = 1.0 / (1.0 + 0.3275911 * 0.5 ** 0.5 * jnp.abs(x))
    e = jnp.exp(-0.5 * (x * x))
    poly = t * (0.127414796 + t * (-0.142248368 + t * (0.7107068705 + t * (-0.7265760135 + t * 0.5307027145))))
    tail = poly * e
    return jnp.where(x >= 0, 1.0 - tail, tail), e


def half_mask(half):
    lane = lax.broadcasted_iota(jnp.int32, (1, 128), 1)
    return (lane < HEAD_SIZE) if half == 0 else (lane >= HEAD_SIZE)


def keep(mask, v):
    return jnp.where(mask, v, jnp.zeros_like(v))


def lanes(part, j):
    start = part * 512 + j * 128
    return pl.ds(start if isinstance(j, int) else pl.multiple_of(start, 128), 128)


def mask_lanes(rows, keys, group):
    lane = lax.broadcasted_iota(jnp.int32, (rows, 128), 1) % HEAD_SIZE
    row = lax.broadcasted_iota(jnp.int32, (rows, 128), 0)
    ones = (lane == row % group).astype(bf16)
    off = (lane < group) & ((lane != row % group) | (row // group >= keys))
    return ones, jnp.where(off, masked_score, 0.0).astype(bf16)


def slot(ref, base, n, size):
    side = 512 // size
    if side == 1:
        return ref.at[base + n]
    n, row, col = n // (side * side), n // side % side, n % side
    return ref.at[base + n, row * size:(row + 1) * size, col * size:(col + 1) * size]


def attend(jobs, size, extra, qkv, o, lse, wide, narrow):
    ones, off = extra
    for i, (rows, j, at) in enumerate(jobs):
        q = qkv[rows, lanes(0, j)] * jnp.asarray(SCALE, bf16)
        k = qkv[rows, lanes(1, j)]
        for half in (0, 1):
            msk = half_mask(half)
            slot(wide, 0, 2 * i + half, size)[...] = mm_nt(jnp.where(msk, k, off), jnp.where(msk, q, ones))
    for i, (rows, j, at) in enumerate(jobs):
        for half in (0, 1):
            s = slot(wide, 0, 2 * i + half, size)[...]
            top = jnp.max(s, 0, keepdims=True)
            e = jnp.exp(s - top)
            mass = over_rows(e)
            slot(narrow, 0, 2 * i + half, size)[...] = (e * (1.0 / mass)).astype(bf16)
            lse[at(2 * j + half)] = top + jnp.log(mass)
    for i, (rows, j, at) in enumerate(jobs):
        v = qkv[rows, lanes(2, j)]
        a, b = (mm_tn(slot(narrow, 0, 2 * i + half, size)[...], v) for half in (0, 1))
        o[rows, lanes(0, j)] = jnp.where(half_mask(0), a, b).astype(bf16)


def attend_back(jobs, size, extra, qkv, o, lse, do, dqkv, wide, narrow):
    ones, off = extra
    head = lax.broadcasted_iota(jnp.int32, (8, 128), 1) // HEAD_SIZE
    pick = (head == lax.broadcasted_iota(jnp.int32, (8, 128), 0)).astype(bf16)
    deltas = []
    for i, (rows, j, at) in enumerate(jobs):
        q = qkv[rows, lanes(0, j)] * jnp.asarray(SCALE, bf16)
        k = qkv[rows, lanes(1, j)]
        v = qkv[rows, lanes(2, j)]
        d = do[rows, lanes(0, j)]
        prod = d.astype(f32) * o[rows, lanes(0, j)].astype(f32)
        high = prod.astype(bf16)
        deltas.append(mm_nt(pick, high) + mm_nt(pick, (prod - high.astype(f32)).astype(bf16)))
        for half in (0, 1):
            msk = half_mask(half)
            slot(wide, 0, 2 * i + half, size)[...] = mm_nt(jnp.where(msk, k, off), jnp.where(msk, q, ones))
            slot(wide, 2, 2 * i + half, size)[...] = mm_nt(v, keep(msk, d))
    for i, (rows, j, at) in enumerate(jobs):
        for half in (0, 1):
            p = jnp.exp(slot(wide, 0, 2 * i + half, size)[...] - lse[at(2 * j + half)])
            slot(narrow, 0, 2 * i + half, size)[...] = p.astype(bf16)
            ds = p * (slot(wide, 2, 2 * i + half, size)[...] - deltas[i][half:half + 1])
            slot(narrow, 2, 2 * i + half, size)[...] = ds.astype(bf16)
    first = half_mask(0)
    for i, (rows, j, at) in enumerate(jobs):
        q = qkv[rows, lanes(0, j)] * jnp.asarray(SCALE, bf16)
        k = qkv[rows, lanes(1, j)]
        d = do[rows, lanes(0, j)]
        p = [slot(narrow, 0, 2 * i + half, size) for half in (0, 1)]
        ds = [slot(narrow, 2, 2 * i + half, size) for half in (0, 1)]
        dq = jnp.where(first, mm_tn(ds[0][...], k), mm_tn(ds[1][...], k)) * SCALE
        dk = jnp.where(first, mm(ds[0][...], q), mm(ds[1][...], q))
        dv = jnp.where(first, mm(p[0][...], d), mm(p[1][...], d))
        dqkv[rows, lanes(0, j)] = dq.astype(bf16)
        dqkv[rows, lanes(1, j)] = dk.astype(bf16)
        dqkv[rows, lanes(2, j)] = dv.astype(bf16)


def loop(n, body, unrolled=False):
    if unrolled:
        for i in range(n):
            body(i)
    else:
        def step(i, carry):
            body(i)
            return carry
        lax.fori_loop(0, n, step, 0)


def project(h, W, qkv):
    qkv[:, 0:1024] = mm(h, flat(W[0])).astype(bf16)
    qkv[:, 1024:1536] = mm(h, flat(W[1, ..., 0:512])).astype(bf16)


def out_proj(W):
    return flat(W[1, ..., 512:1024])


def put(ref, index, value):
    ref[index] = ref[index] + value.reshape(ref.at[index].shape)


def clear(ref):
    def rows(i):
        ref[i // 4, i // 2 % 2, i % 2] = jnp.zeros(ref.shape[3:], f32)
    loop(8, rows)


LEFT, RIGHT = slice(0, 512), slice(512, 1024)
PART_0, PART_1, PART_P = slice(0, 384), slice(384, 768), slice(768, 1024)


class Place:
    def __init__(self, W):
        self.t, self.w, self.W = lax.axis_index("task"), lax.axis_index("wide"), W
        self.x, self.c = self.t // 2, self.t % 2
        self.z, self.y = self.w // 2, self.w % 2

    def barrier(self, direct):
        peers = [(self.t, (self.w + i) % self.W) for i in range(1, self.W)]
        if direct:
            peers += [((self.t + i) % 4, self.w) for i in (1, 2, 3)]
        bar = pltpu.get_barrier_semaphore()
        for peer in peers:
            pl.semaphore_signal(bar, inc=1, device_id=peer, device_id_type=MESH)
        pl.semaphore_wait(bar, len(peers))

    def other(self, axis):
        if axis == "c":
            return (self.t + 1 - 2 * self.c, self.w)
        if axis == "x":
            return ((self.t + 2) % 4, self.w)
        return (self.t, self.w + 1 - 2 * self.y)

    def along_z(self, step):
        return (self.t, (self.w + 2 * step) % 8)


def remote(src, dst, sems, device):
    return pltpu.make_async_remote_copy(
        src_ref=src, dst_ref=dst, send_sem=sems.at[0], recv_sem=sems.at[1], device_id=device, device_id_type=MESH
    )


class Exchange:
    def __init__(self, place, src, dst, sems):
        me, W = place.w, place.W
        self.copies = []
        for i in range(W - 1, 0, -1):
            peer = (me + i) % W
            self.copies.append(remote(src(peer), dst(me), sems.at[i], (place.t, peer)))
        self.copies.append(pltpu.make_async_copy(src(me), dst(me), sems.at[0, 0]))

    def start(self):
        for copy in self.copies:
            copy.start()

    def wait(self):
        for copy in self.copies:
            copy.wait()


class Gather:
    def __init__(self, place, ref, order, sems, chain):
        x, c, z, y = place.x, place.c, place.z, place.y
        self.z, self.stages = z, []
        block = lambda at: ref.at[:, x, c, at, y]
        if chain:
            up, down = place.along_z(1), place.along_z(3)
            for h in (1, 2, 3):
                self.stages.append([
                    (remote(block((z - h + 5) % 4), block((z - h + 5) % 4), sems.at[h - 1], up), (z < 3) & (z >= h - 1), z >= h),
                    (remote(block((z + h + 3) % 4), block((z + h + 3) % 4), sems.at[h + 2], down), (z > 0) & (z <= 4 - h), z <= 3 - h),
                ])
        else:
            self.stages.append([(remote(block(z), block(z), sems.at[s], place.along_z(s)), None, None) for s in (1, 2, 3)])
        line = ref.at[:, x, c, :, y]
        plane = ref.at[:, x, c] if order == "yx" else ref.at[:, :, c, :, y]
        half = ref.at[:, :, c]
        for n, (part, axis) in enumerate(((line, order[0]), (plane, order[1]), (half, "c"))):
            self.stages.append([(remote(part, part, sems.at[6 + n], place.other(axis)), None, None)])

    def start(self, stage):
        for copy, sends, _ in self.stages[stage]:
            if sends is None:
                copy.start()
            else:
                pl.when(sends)(copy.start)

    def wait(self, stage):
        for copy, sends, receives in self.stages[stage]:
            if sends is None:
                copy.wait()
            else:
                pl.when(sends)(copy.wait_send)
                pl.when(receives)(copy.wait_recv)

    def pull(self, stage):
        if stage > 0:
            self.wait(stage - 1)
        if stage < len(self.stages):
            self.start(stage)


class SumAll:
    def __init__(self, place, slots, sems):
        peers = [[place.along_z(s) for s in (1, 2, 3)], [place.other("y")], [place.other("x")], [place.other("c")]]
        self.slots, self.stages, n = slots, [], 0
        for group in peers:
            stage = []
            for peer in group:
                stage.append((n, peer))
                n += 1
            self.stages.append(stage)
        self.copies = [
            [remote(slots.at[s], slots.at[4 + n], sems.at[n], peer) for n, peer in stage]
            for s, stage in enumerate(self.stages)
        ]

    def start(self, stage, value=None):
        if stage == 0:
            self.slots[0] = value
        for copy in self.copies[stage]:
            copy.start()

    def wait(self, stage):
        total = self.slots[stage].astype(f32)
        for copy, (n, _) in zip(self.copies[stage], self.stages[stage]):
            copy.wait()
            total = total + self.slots[4 + n].astype(f32)
        if stage < 3:
            self.slots[stage + 1] = total.astype(self.slots.dtype)
        return total


class SumSmall:
    def __init__(self, place, slots, sems):
        self.slots = slots
        t, w = place.t, place.w
        self.one = [remote(slots.at[0], slots.at[1 + i], sems.at[i], (t, (w + i) % 8)) for i in range(1, 8)]
        self.two = [remote(slots.at[1], slots.at[8 + i], sems.at[7 + i], ((t + i) % 4, w)) for i in range(1, 4)]

    def start(self, value):
        self.slots[0] = value
        for copy in self.one:
            copy.start()

    def turn(self):
        total = self.slots[0]
        for i, copy in enumerate(self.one):
            copy.wait()
            total = total + self.slots[2 + i]
        self.slots[1] = total
        for copy in self.two:
            copy.start()

    def finish(self):
        total = self.slots[1]
        for i, copy in enumerate(self.two):
            copy.wait()
            total = total + self.slots[9 + i]
        return total


SUM_SLOTS = 10


class Scatter:
    def __init__(self, place, grad, order, bufs, sems):
        self.p, self.grad, self.order, self.sems = place, grad, order, sems
        self.recv, self.s1, self.r1, self.r2, self.r3 = bufs
        self.s2 = self.s3 = self.s1.at[:, 0] if order == "xy" else self.s1.at[0]
        x, c, z, y = place.x, place.c, place.z, place.y
        self.core = remote(grad.at[:, 1 - c], self.recv, sems.at[0], place.other("c"))
        first, second = ("x", "y") if order == "xy" else ("y", "x")
        self.one = remote(self.s1, self.r1, sems.at[1], place.other(first))
        self.two = remote(self.s2, self.r2, sems.at[2], place.other(second))
        self.three = [
            remote(self.s3.at[(z + s) % 4], self.r3.at[s - 1], sems.at[2 + s], place.along_z(s)) for s in (1, 2, 3)
        ]

    def step(self, stage):
        x, c, z, y = self.p.x, self.p.c, self.p.z, self.p.y
        xy = self.order == "xy"
        sums = self.recv
        if stage == 0:
            self.core.start()
        elif stage == 1:
            self.core.wait()
            sums[...] = sums[...] + self.grad[:, c]
            self.s1[...] = (sums[1 - x] if xy else sums[:, :, 1 - y]).astype(bf16)
            self.one.start()
        elif stage == 2:
            self.one.wait()
            if xy:
                sums[x] = sums[x] + self.r1[...].astype(f32)
                self.s2[...] = sums[x, :, 1 - y].astype(bf16)
            else:
                sums[:, :, y] = sums[:, :, y] + self.r1[...].astype(f32)
                self.s2[...] = sums[1 - x, :, y].astype(bf16)
            self.two.start()
        elif stage == 3:
            self.two.wait()
            sums[x, :, y] = sums[x, :, y] + self.r2[...].astype(f32)
            self.s3[...] = sums[x, :, y].astype(bf16)
            for copy in self.three:
                copy.start()
        else:
            total = sums[x, z, y]
            for i, copy in enumerate(self.three):
                copy.wait()
                total = total + self.r3[i].astype(f32)
            return total


def scatter_bufs(rows, cols, order):
    first = (4, 2, rows, cols) if order == "xy" else (2, 4, rows, cols)
    return [
        pltpu.VMEM((2, 4, 2, rows, cols), f32),
        pltpu.VMEM(first, bf16), pltpu.VMEM(first, bf16),
        pltpu.VMEM((4, rows, cols), bf16), pltpu.VMEM((3, rows, cols), bf16),
    ]


ORDERS = ("yx", "xy")


VECTORS = 9


def layer_kernel(direct, W, groups, *refs):
    refs = list(refs)
    take = lambda n: [refs.pop(0) for _ in range(n)]
    count_s, count_f, tok, cot = take(4)
    if direct:
        sq, sp, fq, fp, up, dn, small = take(7)
    else:
        A, B, C, D, vec_in = take(5)
    result, gin = take(2)
    if direct:
        out_sq, out_sp, out_fq, out_fp, out_up, out_dn = take(6)
        out_small = take(10)
    else:
        gA, gB, gC, gD, gvec_out = take(5)
    arr, cots, leave, gleave, grecv, qkv_s, o_s, lse_s = take(8)
    vec, gvec, qkv, o, lse, stream, h2, wide, narrow = take(9)
    dqkv, do = qkv, h2
    dout, dh2 = wide.at[2], wide.at[3]
    if direct:
        A, B, C, D, gB, gC, gD = take(7)
        gA = gC
        vslots, eslots, lslots, wsems, vsems, esems, tsems, ssems = take(8)
        bufs = [take(5) for _ in range(12)]
    xsems, lsems = take(2)
    p = Place(W)
    t, w = p.t, p.w
    rank = t * 8 + w
    block_rows = W * TILE

    def of_peer(ref, m):
        return lambda peer: ref.at[m, peer * groups // W, pl.ds(peer * groups % W, groups)]

    of_cot = lambda m: lambda peer: cot.at[m, pl.ds(peer * groups, groups)]
    by_feature = lambda ref, m: lambda peer: ref.at[m, :, peer]
    by_sample = lambda ref, m: lambda peer: ref.at[m, pl.ds(peer * groups, groups)]
    cot_move = lambda m: Exchange(p, of_cot(m), by_feature(cots, m), xsems.at[m])
    first_move = lambda m: Exchange(p, of_peer(leave, m), by_feature(arr, m), xsems.at[2 + m])
    out_move = lambda m: Exchange(p, by_feature(leave, m), by_sample(result, m), xsems.at[4 + m])
    back_move = lambda m: Exchange(p, by_feature(gleave, m), by_sample(grecv, m), xsems.at[6 + m])
    gin_move = lambda m: pltpu.make_async_copy(grecv.at[m], gin.at[m], lsems.at[m])
    GA = GB = GC = GD = SP = SQ0 = SQ1 = SB = SC = SD = ()
    if direct:
        unit = lambda ref, u, n, order, chain: Gather(p, ref.at[u:u + 1], order, wsems.at[n], chain)
        GA = [unit(A, 0, 0, "yx", False), unit(A, 1, 1, "xy", False)]
        GB = [Gather(p, B, "yx", wsems.at[2], True)]
        GC = [unit(C, 0, 3, "yx", True), unit(C, 1, 4, "xy", True)]
        GD = [unit(D, 0, 5, "yx", True), unit(D, 1, 6, "xy", True)]
        scatters = [
            Scatter(p, ref.at[(u, *[slice(None)] * 5, cols)], ORDERS[u], bufs[2 * n + u], ssems.at[2 * n + u])
            for n, (ref, cols) in enumerate(
                ((gA, PART_P), (gA, PART_0), (gA, PART_1), (gB, slice(0, 1024)), (gC, slice(0, 1024)), (gD, slice(0, 256)))
            ) for u in (0, 1)
        ]
        SP, SQ0, SQ1, SB, SC, SD = (scatters[2 * n:2 * n + 2] for n in range(6))

    def pull(group, stage):
        for g in group:
            g.pull(stage)

    def push(group, stage):
        return [s.step(stage) for s in group]

    def serve(point, actions):
        for at, action in (actions.items() if direct else ()):
            if isinstance(point, int):
                if point == at:
                    action()
                continue

            @pl.when(point == at)
            def _():
                action()

    p.barrier(direct)
    if direct:
        at = (p.x, p.c, p.z, p.y)
        A[(0, *at)] = sq[:, 0:1024]
        A[(1, *at, slice(None), LEFT)] = sq[:, 1024:1536]
        A[(1, *at, slice(None), RIGHT)] = sp[...]
        pull(GA, 0)
        n, l = (lax.broadcasted_iota(jnp.int32, (16, 256), d) for d in (0, 1))
        short = (l < VECTORS * 16) & (l // 16 == n)
        long = (l >= VECTORS * 16) & (l < VECTORS * 16 + 64) & (n == VECTORS + rank // 8)
        spread = jnp.where(short | long, jnp.broadcast_to(small[...], (16, 256)), jnp.zeros((16, 256), bf16))
        l, j = (lax.broadcasted_iota(jnp.int32, (256, 512), d) for d in (0, 1))
        goal = jnp.where(l < VECTORS * 16, rank * 16 + l % 16, rank % 8 * 64 + l - VECTORS * 16)
        both = SumAll(p, vslots, vsems)
        both.start(0, mm(spread, (j == goal).astype(bf16)).astype(bf16))
        B[(0, *at)] = fq[:, 0:1024]
        B[(1, *at, slice(None), LEFT)] = fq[:, 1024:1536]
        B[(1, *at, slice(None), RIGHT)] = fp[...]
        for u in (0, 1):
            C[(u, *at)] = up[:, 1024 * u:1024 * u + 1024]
            D[(u, *at)] = dn[:, 256 * u:256 * u + 256]
    for ref in (gB, gC, gD):
        clear(ref)
    gvec[...] = jnp.zeros(gvec.shape, f32)
    if direct:
        both.wait(0)
        both.start(1)
        pull(GA, 1)
        pull(GB, 0)
        cot_move(0).start()
        both.wait(1)
        both.start(2)
        pull(GB, 1)
        pull(GC, 0)
        pull(GA, 2)
        pull(GB, 2)
        pull(GC, 1)
        pull(GD, 0)
        both.wait(2)
        both.start(3)
        pull(GB, 3)
        pull(GC, 2)
        pull(GD, 1)
        pull(GA, 3)
        rows = both.wait(3)
        for n in range(16):
            vec[n] = rows[n:n + 1]
        pull(GC, 3)
        pull(GD, 2)
        pull(GB, 4)
        pull(GA, 4)
    else:
        cot_move(0).start()
        for n in range(16):
            vec[n] = vec_in[n:n + 1, :].astype(f32)
    row = lambda n: vec[n]
    everything = slice(None)
    whole_rows = lambda n: [(everything, n, lambda h: h)]
    moving = {
        0: lambda: pull(GD, 3),
        2: lambda: pull(GC, 4),
        5: lambda: pull(GB, 5),
        8: lambda: (pull(GB, 6), pull(GD, 4)),
    }

    def samples(m):
        extra = mask_lanes(512, count_s[0, m], 1)
        unit, _ = normed(tok[m].astype(f32))
        project((unit * row(0) + row(1)).astype(bf16), A, qkv_s.at[m])

        def pair(n):
            attend(whole_rows(n), 512, extra, qkv_s.at[m], o_s.at[m], lse_s.at[m], wide, narrow)
            serve(m * 5 + n, moving)

        loop(PAIRS, pair)
        branch = mm(o_s[m], out_proj(A)) + row(2)
        leave[m] = (tok[m].astype(f32) + branch).astype(bf16).reshape(leave.shape[1:])
        first_move(m).start()
        serve(m * 5 + 4, moving)

    def features(m):
        extra = mask_lanes(block_rows, count_f[0, m], TILE)

        def blocks(body):
            def jobs_of(g, pairs):
                rows = pl.ds(g * block_rows, block_rows)
                return [(rows, n, lambda h: (h, everything, rows)) for n in pairs]

            if block_rows == 128:
                body([job for g in range(groups) for job in jobs_of(g, range(PAIRS))], block_rows)
            else:
                for g in range(groups):
                    loop(PAIRS, lambda n: body(jobs_of(g, [n]), block_rows))

        first_move(m).wait()
        unit, _ = normed(flat(arr[m]).astype(f32))
        project((unit * row(3) + row(4)).astype(bf16), B, qkv)
        serve(m, {0: lambda: pull(GC, 5)})
        blocks(lambda jobs, size: attend(jobs, size, extra, qkv, o, lse, wide, narrow))
        s2 = flat(arr[m]).astype(f32) + mm(o[...], out_proj(B)) + row(5)
        stream[...] = s2
        unit, _ = normed(s2)
        h2[...] = (unit * row(6) + row(7)).astype(bf16)
        serve(m, {0: lambda: (pull(GC, 6), pull(GD, 5), pull(GD, 6))})
        cot_move(m).wait()
        pl.when(m == 0)(lambda: cot_move(1).start())

        def chunk(n):
            half = n // 2
            cols = pl.ds(pl.multiple_of((n % 2) * 512, 512), 512)
            upw = C[half, :, :, :, :, :, cols].reshape(512, 512)
            d0 = D[0, n // 2, n % 2].reshape(512, 256)
            d1 = D[1, n // 2, n % 2].reshape(512, 256)
            g16 = flat(cots[m])
            wide[0] = mm(h2[...], upw) + vec[VECTORS + n]
            wide[1] = mm_nt(g16[:, 0:256], d0) + mm_nt(g16[:, 256:512], d1)
            total = jnp.zeros((8, 512), f32)
            for r in range(0, 512, 64):
                part = slice(r, r + 64)
                raised = wide[0, part]
                phi, e = gelu_parts(raised)
                narrow[0, part] = (raised * phi).astype(bf16)
                draised = (wide[1, part] * (phi + raised * e * (0.5 / jnp.pi) ** 0.5)).astype(bf16)
                narrow[1, part] = draised
                total = total + jnp.sum(draised.astype(f32).reshape(8, 8, 512), 0)
            gvec[VECTORS + n] += over_rows(total)
            a0, a1, b0 = mm(narrow[0], d0), mm(narrow[0], d1), mm_nt(narrow[1], upw)

            @pl.when(n == 0)
            def _():
                dout[:, 0:256] = a0
                dout[:, 256:512] = a1
                dh2[...] = b0

            @pl.when(n > 0)
            def _():
                dout[:, 0:256] += a0
                dout[:, 256:512] += a1
                dh2[...] += b0

            put(gC, (half, *[everything] * 5, cols), mm_tn(h2[...], narrow[1]))
            put(gD, (0, n // 2, n % 2), mm_tn(narrow[0], g16[:, 0:256]))
            put(gD, (1, n // 2, n % 2), mm_tn(narrow[0], g16[:, 256:512]))

        loop(4, chunk)
        leave[m] = (stream[...] + dout[...] + row(8)).astype(bf16).reshape(leave.shape[1:])
        out_move(m).start()
        serve(m, {1: lambda: (push(SC, 0), push(SD, 0))})
        cot16 = flat(cots[m]).astype(f32)
        gvec[8] += over_rows(cot16)
        unit, scale = normed(stream[...])
        dh = dh2[...]
        gvec[6] += over_rows(dh * unit)
        gvec[7] += over_rows(dh)
        g2 = cot16 + normed_back(dh, unit, scale, row(6))
        stream[...] = g2
        gy = g2.astype(bf16)
        put(gB, (1, Ellipsis, RIGHT), mm_tn(o[...], gy))
        gvec[5] += over_rows(gy.astype(f32))
        do[...] = mm_nt(gy, out_proj(B)).astype(bf16)
        serve(m, {1: lambda: push(SC, 1)})
        blocks(lambda jobs, size: attend_back(jobs, size, extra, qkv, o, lse, do, dqkv, wide, narrow))
        serve(m, {1: lambda: push(SD, 1)})
        unit, scale = normed(flat(arr[m]).astype(f32))
        h = (unit * row(3) + row(4)).astype(bf16)
        dh = mm_nt(dqkv[:, 0:1024], flat(B[0])) + mm_nt(dqkv[:, 1024:1536], flat(B[1, ..., LEFT]))
        gleave[m] = (stream[...] + normed_back(dh, unit, scale, row(3))).astype(bf16).reshape(gleave.shape[1:])
        back_move(m).start()
        gvec[3] += over_rows(dh * unit)
        gvec[4] += over_rows(dh)
        put(gB, 0, mm_tn(h, dqkv[:, 0:1024]))
        put(gB, (1, Ellipsis, LEFT), mm_tn(h, dqkv[:, 1024:1536]))

    def finish_cd():
        done = push(SC, 4) + push(SD, 4)
        out_up[:, 0:1024], out_up[:, 1024:2048], out_dn[:, 0:256], out_dn[:, 256:512] = done

    def finish_b():
        done = push(SB, 4)
        out_fq[:, 0:1024] = done[0]
        out_fq[:, 1024:1536] = done[1][:, LEFT]
        out_fp[...] = done[1][:, RIGHT]

    def fold(first, last):
        parts = [gvec[n][:, 128 * k:128 * k + 128] for n in range(first, last) for k in range(4)]
        pad = -len(parts) % 8
        return jnp.concatenate(parts + ([jnp.zeros((pad, 128), f32)] if pad else []), 0)

    early = SumSmall(p, eslots, esems) if direct else None
    late = SumSmall(p, lslots, tsems) if direct else None
    back_steps = {
        0: lambda: push(SB, 1),
        1: lambda: push(SC, 2),
        2: lambda: push(SD, 2),
        3: lambda: (push(SC, 3), push(SB, 2)),
        5: lambda: (push(SD, 3), early.start(fold(2, 13))),
        6: lambda: push(SP, 0),
        7: lambda: (push(SB, 3), push(SP, 1)),
        8: lambda: finish_cd(),
    }

    def samples_back(m):
        extra = mask_lanes(512, count_s[0, m], 1)
        back_move(m).wait()
        gy = flat(grecv[m])
        for u in (0, 1):
            put(gA, (u, *[everything] * 5, PART_P), mm_tn(o_s[m], gy[:, 256 * u:256 * u + 256]))
        gvec[2] += over_rows(gy.astype(f32))
        do[...] = mm_nt(gy, out_proj(A)).astype(bf16)
        serve(m * 5, {5: back_steps.get(5)})
        unit, _ = normed(tok[m].astype(f32))
        h[...] = (unit * row(0) + row(1)).astype(bf16)
        here = qkv_s.at[m]

        def two_pairs(r):
            def pair(n):
                attend_back(whole_rows(2 * r + n), 512, extra, here, o_s.at[m], lse_s.at[m], do, here, wide, narrow)
                serve(m * 5 + 2 * r + n + m, {k: f for k, f in back_steps.items() if k != 5})

            loop(2, pair)
            cols = lambda part: here[:, pl.ds(pl.multiple_of(512 * part + 256 * r, 256), 256)]
            grad = mm_tn(h[...], jnp.concatenate([cols(0), cols(1), cols(2)], 1))
            for u in (0, 1):
                lane = pl.ds(pl.multiple_of(384 * r, 128), 384)
                put(gA, (u, *[everything] * 5, lane), grad[:, 384 * u:384 * u + 384])
            serve(m * 2 + r, {2: lambda: push(SQ0, 0), 3: lambda: (push(SQ0, 1), push(SQ1, 0))})

        loop(2, two_pairs)

    def samples_end(m):
        unit, scale = normed(tok[m].astype(f32))
        dh = mm_nt(qkv_s[m, :, 0:1024], flat(A[0])) + mm_nt(qkv_s[m, :, 1024:1536], flat(A[1, ..., LEFT]))
        gvec[0] += over_rows(dh * unit)
        gvec[1] += over_rows(dh)
        grecv[m] = (flat(grecv[m]).astype(f32) + normed_back(dh, unit, scale, row(0))).astype(bf16).reshape(grecv.shape[1:])
        gin_move(m).start()
        serve(m, {0: lambda: (push(SP, 2), push(SQ1, 1)), 1: lambda: (push(SQ0, 2), push(SP, 3))})

    h = o
    loop(2, samples)
    loop(2, features)
    push(SB, 0)
    clear(gA)
    loop(2, samples_back)
    if direct:
        early.turn()
    loop(2, samples_end)
    if direct:
        late.start(fold(0, 2))
        push(SQ1, 2)
        push(SQ0, 3)
        finish_b()
        sums = early.finish()
        late.turn()
        push(SQ1, 3)
        for u, part in enumerate(push(SP, 4)):
            out_sp[:, 256 * u:256 * u + 256] = part
        l, j = (lax.broadcasted_iota(jnp.int32, (128, 128), d) for d in (0, 1))

        def own(rows, start, size):
            return lax.dot_general(
                jnp.concatenate(rows, 0), (l == start + j).astype(f32), (((1,), (0,)), ((), ())),
                precision=lax.Precision.HIGHEST, preferred_element_type=f32,
            )[:, 0:size]

        def row_at(v, at):
            return over_rows(keep(lax.broadcasted_iota(jnp.int32, v.shape, 0) == at, v))

        zero = jnp.zeros((1, 128), f32)
        mine = own([row_at(sums, 4 * n + rank // 8) for n in range(7)] + [zero], rank % 8 * 16, 16)
        for n in range(7):
            out_small[2 + n][...] = mine[n:n + 1]
        long = row_at(sums, 4 * (7 + rank // 8) + rank % 8 // 2)
        out_small[VECTORS][...] = own([long] + [zero] * 7, rank % 2 * 64, 64)[0:1]
        sums = late.finish()
        mine = own([row_at(sums, 4 * n + rank // 8) for n in range(2)] + [zero] * 6, rank % 8 * 16, 16)
        for n in range(2):
            out_small[n][...] = mine[n:n + 1]
        for r, group in enumerate((SQ0, SQ1)):
            a, b = push(group, 4)
            q, k, v = 256 * r, 512 + 256 * r, 1024 + 256 * r
            out_sq[:, q:q + 256] = a[:, 0:256]
            out_sq[:, k:k + 128] = a[:, 256:384]
            out_sq[:, k + 128:k + 256] = b[:, 0:128]
            out_sq[:, v:v + 256] = b[:, 128:384]
    else:
        for n in range(VECTORS + 4):
            gvec_out[n:n + 1, :] = gvec[n]
        gvec_out[VECTORS + 4:, :] = jnp.zeros((3, 512), f32)
    for m in (0, 1):
        out_move(m).wait()
        gin_move(m).wait()


def copy_kernel(*refs):
    n = len(refs) // 2
    for source, goal in zip(refs[:n], refs[n:]):
        goal[...] = source[...]


def shards(mesh, *args):
    (tokens, cotangent, sample_count, feature_count, sample_gain, sample_shift, sample_qkv, sample_proj, sample_bias,
     feature_gain, feature_shift, feature_qkv, feature_proj, feature_bias, mlp_gain, mlp_shift, up_weight, up_bias,
     down_weight, down_bias) = args
    T, W = mesh.shape["task"], mesh.shape["wide"]
    micro, _, length, _, width = tokens.shape
    groups = length // W // TILE
    direct = sample_qkv.shape[0] == TILE and T == 4 and W == 8
    axes = ("task", "wide")
    by_sample = (micro, groups, W, TILE, width)
    by_feature = (micro, W * groups, TILE, width)
    columns = lambda v: v.transpose(0, 1, 3, 2, 4)
    tok = columns(tokens).reshape(micro, length, width)
    cot = columns(cotangent).reshape(by_feature)
    vectors = (sample_gain, sample_shift, sample_bias, feature_gain, feature_shift, feature_bias, mlp_gain, mlp_shift, down_bias)
    V = pl.BlockSpec(memory_space=pltpu.VMEM)
    S = pl.BlockSpec(memory_space=pltpu.SMEM)
    H = pl.BlockSpec(memory_space=pl.ANY)
    sds = lambda shape, dtype=bf16: jax.ShapeDtypeStruct(shape, dtype)
    dma = lambda *shape: pltpu.SemaphoreType.DMA(shape)
    flat_of = lambda n, kind: pltpu.VMEM((length, n * width), kind)
    logs = pltpu.VMEM((HEADS, 1, length), f32)
    square, tall = (2, *SPLIT, TILE, 1024), (2, *SPLIT, 64, 256)
    scratch = [pltpu.VMEM(by_sample, bf16)] * 4 + [
        pltpu.VMEM(by_feature, bf16), pltpu.VMEM((micro, length, 3 * width), bf16), pltpu.VMEM((micro, length, width), bf16),
        pltpu.VMEM((micro, HEADS, 1, length), f32), pltpu.VMEM((16, 1, width), f32), pltpu.VMEM((16, 1, width), f32),
        flat_of(3, bf16), flat_of(1, bf16), logs, flat_of(1, f32), flat_of(1, bf16),
        pltpu.VMEM((4, length, width), f32), pltpu.VMEM((4, length, width), bf16),
    ]
    matrices = (sample_qkv, sample_proj, feature_qkv, feature_proj, up_weight, down_weight)
    outs = [sds(by_feature), sds(by_feature)]
    counts = (sample_count.T, feature_count.T)
    if direct:
        small = jnp.concatenate([*vectors, up_bias, jnp.zeros(48, bf16)]).reshape(1, 256)
        ins = (*matrices, small)
        outs += [sds(v.shape, f32) for v in matrices] + [sds((1, v.shape[0]), f32) for v in (*vectors, up_bias)]
        scratch += [pltpu.VMEM(square, bf16)] * 3 + [pltpu.VMEM(tall, bf16)] + [pltpu.VMEM(square, f32)] * 2 + [pltpu.VMEM(tall, f32)]
        scratch += [pltpu.VMEM((SUM_SLOTS, 16, width), bf16), pltpu.VMEM((12, 48, 128), f32), pltpu.VMEM((12, 8, 128), f32)]
        scratch += [dma(7, 9, 2), dma(6, 2), dma(11, 2), dma(11, 2), dma(12, 6, 2)]
        for rows, cols in ((TILE, 256), (TILE, 384), (TILE, 384), (TILE, 1024), (TILE, 1024), (64, 256)):
            for order in ORDERS:
                scratch += scatter_bufs(rows, cols, order)
    else:
        gather = lambda v: lax.all_gather(v, axes, axis=0, tiled=True)
        sq, sp, fq, fp, up, dn = map(gather, matrices)
        pair = lambda q, o: jnp.stack([q[:, 0:1024], jnp.concatenate([q[:, 1024:], o], 1)]).reshape(square)
        C = jnp.stack([up[:, 0:1024], up[:, 1024:]]).reshape(square)
        D = jnp.stack([dn[:, 0:256], dn[:, 256:]]).reshape(tall)
        rest = [gather(up_bias).reshape(4, width), jnp.zeros((3, width), bf16)]
        ins = (pair(sq, sp), pair(fq, fp), C, D, jnp.concatenate([jnp.stack([gather(v) for v in vectors]), *rest], 0))
        outs += [sds(square, f32)] * 3 + [sds(tall, f32), sds((16, width), f32)]
    done = pl.pallas_call(
        lambda *refs: layer_kernel(direct, W, groups, *refs), name="layer",
        in_specs=[S, S, V, H] + [V] * len(ins), out_specs=[H, H] + [V] * (len(outs) - 2), out_shape=outs,
        scratch_shapes=scratch + [dma(8, W, 2), dma(2)],
        compiler_params=pltpu.CompilerParams(collective_id=1, has_side_effects=True, vmem_limit_bytes=63 * MIB),
    )(*counts, tok, cot, *ins)
    if direct:
        done = pl.pallas_call(
            copy_kernel, name="hand_out", in_specs=[V] * len(outs), out_specs=[V] * len(outs), out_shape=outs,
        )(*done)
    restore = lambda v: columns(v.reshape(micro, 1, 1, length, width))
    output, input_grad = restore(done[0]), restore(done[1])
    if direct:
        g_sq, g_sp, g_fq, g_fp, g_up, g_dn = done[2:8]
        g = [v.reshape(-1) for v in done[8:18]]
    else:
        gA, gB, gC, gD, gv = done[2:7]
        two = lambda v: v.reshape(2, -1, v.shape[-1])
        joined = lambda v: jnp.concatenate([two(v)[0], two(v)[1]], 1)
        b = joined(gB)
        q, k, v = [], [], []
        for part in (PART_0, PART_1):
            one, two_ = two(gA)[0][:, part], two(gA)[1][:, part]
            q.append(one[:, 0:256])
            k += [one[:, 256:384], two_[:, 0:128]]
            v.append(two_[:, 128:384])
        a = jnp.concatenate([*q, *k, *v, two(gA)[0][:, PART_P], two(gA)[1][:, PART_P]], 1)
        scatter = lambda v: lax.psum_scatter(v, axes, scatter_dimension=0, tiled=True)
        g_sq, g_sp, g_fq, g_fp, g_up, g_dn = map(scatter, (a[:, :1536], a[:, 1536:], b[:, :1536], b[:, 1536:], joined(gC), joined(gD)))
        g = [scatter(gv[n]) for n in range(VECTORS)] + [scatter(gv[VECTORS:VECTORS + 4].reshape(-1))]
    return (output, input_grad, g[0], g[1], g_sq, g_sp, g[2], g[3], g[4], g_fq, g_fp, g[5], g[6], g[7], g_up, g[9], g_dn, g[8])


def solution(mesh):
    rows = P(("task", "wide"))
    table = P(("task", "wide"), None)
    data = P(None, "task", None, "wide", None)
    params = (rows, rows, table, table, rows, rows, rows, table, table, rows, rows, rows, table, rows, table, rows)
    counts = P(None, "task")

    def run(*args):
        return shards(mesh, *args)

    return jax.shard_map(
        run, mesh=mesh, in_specs=(data, data, counts, counts) + params, out_specs=(data, data) + params, check_vma=False
    )
```

```python
import jax
import jax.numpy as jnp
from jax import lax
from jax.experimental import pallas as pl
from jax.experimental.pallas import tpu as pltpu
from jax.sharding import PartitionSpec as P

HEADS = 8
HEAD_SIZE = 64
PAIRS = HEADS // 2
SCALE = HEAD_SIZE ** -0.5
TILE = 16
SPLIT = (2, 2, 4, 2)

epsilon = 1e-05
masked_score = -1e30
f32, bf16 = jnp.float32, jnp.bfloat16
MESH = pl.DeviceIdType.MESH
MIB = 1 << 20


def mm(a, b):
    return lax.dot_general(a, b, (((1,), (0,)), ((), ())), preferred_element_type=f32)


def mm_nt(a, b):
    return lax.dot_general(a, b, (((1,), (1,)), ((), ())), preferred_element_type=f32)


def mm_tn(a, b):
    return lax.dot_general(a, b, (((0,), (0,)), ((), ())), preferred_element_type=f32)


def flat(value):
    return value.reshape(-1, value.shape[-1])


def normed(v):
    centred = v - jnp.mean(v, -1, keepdims=True)
    scale = lax.rsqrt(jnp.mean(centred * centred, -1, keepdims=True) + epsilon)
    return centred * scale, scale


def normed_back(grad, unit, scale, gain):
    t = grad * gain
    return scale * (t - jnp.mean(t, -1, keepdims=True) - unit * jnp.mean(t * unit, -1, keepdims=True))


def over_rows(v):
    return jnp.sum(v, 0, keepdims=True)


def gelu_parts(x):
    t = 1.0 / (1.0 + 0.3275911 * 0.5 ** 0.5 * jnp.abs(x))
    e = jnp.exp(-0.5 * (x * x))
    poly = t * (0.127414796 + t * (-0.142248368 + t * (0.7107068705 + t * (-0.7265760135 + t * 0.5307027145))))
    tail = poly * e
    return jnp.where(x >= 0, 1.0 - tail, tail), e


def half_mask(half):
    lane = lax.broadcasted_iota(jnp.int32, (1, 128), 1)
    return (lane < HEAD_SIZE) if half == 0 else (lane >= HEAD_SIZE)


def keep(mask, v):
    return jnp.where(mask, v, jnp.zeros_like(v))


def lanes(part, j):
    start = part * 512 + j * 128
    return pl.ds(start if isinstance(j, int) else pl.multiple_of(start, 128), 128)


def mask_lanes(rows, keys, group):
    lane = lax.broadcasted_iota(jnp.int32, (rows, 128), 1) % HEAD_SIZE
    row = lax.broadcasted_iota(jnp.int32, (rows, 128), 0)
    ones = (lane == row % group).astype(bf16)
    off = (lane < group) & ((lane != row % group) | (row // group >= keys))
    return ones, jnp.where(off, masked_score, 0.0).astype(bf16)


def slot(ref, base, n, size):
    side = 512 // size
    if side == 1:
        return ref.at[base + n]
    n, row, col = n // (side * side), n // side % side, n % side
    return ref.at[base + n, row * size:(row + 1) * size, col * size:(col + 1) * size]


def attend(jobs, size, extra, qkv, o, lse, wide, narrow, after=lambda phase: None):
    ones, off = extra
    for i, (rows, j, at) in enumerate(jobs):
        q = qkv[rows, lanes(0, j)] * jnp.asarray(SCALE, bf16)
        k = qkv[rows, lanes(1, j)]
        for half in (0, 1):
            msk = half_mask(half)
            slot(wide, 0, 2 * i + half, size)[...] = mm_nt(jnp.where(msk, k, off), jnp.where(msk, q, ones))
    after(0)
    for i, (rows, j, at) in enumerate(jobs):
        for half in (0, 1):
            s = slot(wide, 0, 2 * i + half, size)[...]
            top = jnp.max(s, 0, keepdims=True)
            e = jnp.exp(s - top)
            mass = over_rows(e)
            slot(narrow, 0, 2 * i + half, size)[...] = (e * (1.0 / mass)).astype(bf16)
            lse[at(2 * j + half)] = top + jnp.log(mass)
    after(1)
    for i, (rows, j, at) in enumerate(jobs):
        v = qkv[rows, lanes(2, j)]
        a, b = (mm_tn(slot(narrow, 0, 2 * i + half, size)[...], v) for half in (0, 1))
        o[rows, lanes(0, j)] = jnp.where(half_mask(0), a, b).astype(bf16)
    after(2)


def attend_back(jobs, size, extra, qkv, o, lse, do, dqkv, wide, narrow):
    ones, off = extra
    head = lax.broadcasted_iota(jnp.int32, (8, 128), 1) // HEAD_SIZE
    pick = (head == lax.broadcasted_iota(jnp.int32, (8, 128), 0)).astype(bf16)
    deltas = []
    for i, (rows, j, at) in enumerate(jobs):
        q = qkv[rows, lanes(0, j)] * jnp.asarray(SCALE, bf16)
        k = qkv[rows, lanes(1, j)]
        v = qkv[rows, lanes(2, j)]
        d = do[rows, lanes(0, j)]
        prod = d.astype(f32) * o[rows, lanes(0, j)].astype(f32)
        high = prod.astype(bf16)
        deltas.append(mm_nt(pick, high) + mm_nt(pick, (prod - high.astype(f32)).astype(bf16)))
        for half in (0, 1):
            msk = half_mask(half)
            slot(wide, 0, 2 * i + half, size)[...] = mm_nt(jnp.where(msk, k, off), jnp.where(msk, q, ones))
            slot(wide, 2, 2 * i + half, size)[...] = mm_nt(v, keep(msk, d))
    for i, (rows, j, at) in enumerate(jobs):
        for half in (0, 1):
            p = jnp.exp(slot(wide, 0, 2 * i + half, size)[...] - lse[at(2 * j + half)])
            slot(narrow, 0, 2 * i + half, size)[...] = p.astype(bf16)
            ds = p * (slot(wide, 2, 2 * i + half, size)[...] - deltas[i][half:half + 1])
            slot(narrow, 2, 2 * i + half, size)[...] = ds.astype(bf16)
    first = half_mask(0)
    for i, (rows, j, at) in enumerate(jobs):
        q = qkv[rows, lanes(0, j)] * jnp.asarray(SCALE, bf16)
        k = qkv[rows, lanes(1, j)]
        d = do[rows, lanes(0, j)]
        p = [slot(narrow, 0, 2 * i + half, size) for half in (0, 1)]
        ds = [slot(narrow, 2, 2 * i + half, size) for half in (0, 1)]
        dq = jnp.where(first, mm_tn(ds[0][...], k), mm_tn(ds[1][...], k)) * SCALE
        dk = jnp.where(first, mm(ds[0][...], q), mm(ds[1][...], q))
        dv = jnp.where(first, mm(p[0][...], d), mm(p[1][...], d))
        dqkv[rows, lanes(0, j)] = dq.astype(bf16)
        dqkv[rows, lanes(1, j)] = dk.astype(bf16)
        dqkv[rows, lanes(2, j)] = dv.astype(bf16)


def loop(n, body, unrolled=False):
    if unrolled:
        for i in range(n):
            body(i)
    else:
        def step(i, carry):
            body(i)
            return carry
        lax.fori_loop(0, n, step, 0)


def project(h, W, qkv):
    qkv[:, 0:1024] = mm(h, flat(W[0])).astype(bf16)
    qkv[:, 1024:1536] = mm(h, flat(W[1, ..., 0:512])).astype(bf16)


def out_proj(W):
    return flat(W[1, ..., 512:1024])


def put(ref, index, value):
    ref[index] = ref[index] + value.reshape(ref.at[index].shape)


def clear(ref):
    def rows(i):
        ref[i // 4, i // 2 % 2, i % 2] = jnp.zeros(ref.shape[3:], f32)
    loop(8, rows)


LEFT, RIGHT = slice(0, 512), slice(512, 1024)
PART_P = slice(768, 1024)
PART_01 = (slice(0, 384), slice(0, 384))
PART_2 = (slice(384, 640), slice(384, 512))
PART_3 = (slice(640, 768), slice(512, 768))


class Place:
    def __init__(self, W):
        self.t, self.w, self.W = lax.axis_index("task"), lax.axis_index("wide"), W
        self.x, self.c = self.t // 2, self.t % 2
        self.z, self.y = self.w // 2, self.w % 2

    def barrier(self, direct):
        peers = [(self.t, (self.w + i) % self.W) for i in range(1, self.W)]
        if direct:
            peers += [((self.t + i) % 4, self.w) for i in (1, 2, 3)]
        bar = pltpu.get_barrier_semaphore()
        for peer in peers:
            pl.semaphore_signal(bar, inc=1, device_id=peer, device_id_type=MESH)
        pl.semaphore_wait(bar, len(peers))

    def other(self, axis):
        if axis == "c":
            return (self.t + 1 - 2 * self.c, self.w)
        if axis == "x":
            return ((self.t + 2) % 4, self.w)
        return (self.t, self.w + 1 - 2 * self.y)

    def along_z(self, step):
        return (self.t, (self.w + 2 * step) % 8)


def remote(src, dst, sems, device):
    return pltpu.make_async_remote_copy(
        src_ref=src, dst_ref=dst, send_sem=sems.at[0], recv_sem=sems.at[1], device_id=device, device_id_type=MESH
    )


class Exchange:
    def __init__(self, place, src, dst, sems):
        me, W = place.w, place.W
        self.copies = []
        for i in range(W - 1, 0, -1):
            peer = (me + i) % W
            self.copies.append(remote(src(peer), dst(me), sems.at[i], (place.t, peer)))
        self.copies.append(pltpu.make_async_copy(src(me), dst(me), sems.at[0, 0]))

    def start(self):
        for copy in self.copies:
            copy.start()

    def wait(self):
        for copy in self.copies:
            copy.wait()


class Gather:
    def __init__(self, place, ref, order, sems):
        x, c, z, y = place.x, place.c, place.z, place.y
        self.stages = []
        up, down = place.along_z(1), place.along_z(3)
        for hop in (1, 2, 3):
            higher, lower = ref.at[:, x, c, (z + hop + 3) % 4, y], ref.at[:, x, c, (z - hop + 5) % 4, y]
            self.stages.append([
                (remote(lower, lower, sems.at[hop - 1], up), (z < 3) & (z >= hop - 1), z >= hop),
                (remote(higher, higher, sems.at[hop + 2], down), (z > 0) & (z <= 4 - hop), z <= 3 - hop),
            ])
        line, half = ref.at[:, x, c, :, y], ref.at[:, :, c]
        plane = ref.at[:, x, c] if order == "yx" else ref.at[:, :, c, :, y]
        for n, (part, axis) in enumerate(((line, order[0]), (plane, order[1]), (half, "c"))):
            self.stages.append([(remote(part, part, sems.at[6 + n], place.other(axis)), None, None)])

    def pull(self, stage):
        if stage > 0:
            for copy, sends, receives in self.stages[stage - 1]:
                if sends is None:
                    copy.wait()
                else:
                    pl.when(sends)(copy.wait_send)
                    pl.when(receives)(copy.wait_recv)
        if stage < 6:
            for copy, sends, receives in self.stages[stage]:
                if sends is None:
                    copy.start()
                else:
                    pl.when(sends)(copy.start)


class SumAll:
    def __init__(self, place, slots, sems):
        peers = [[place.along_z(s) for s in (1, 2, 3)], [place.other("y")], [place.other("x")], [place.other("c")]]
        self.slots, self.stages, n = slots, [], 0
        for group in peers:
            stage = []
            for peer in group:
                stage.append((n, peer))
                n += 1
            self.stages.append(stage)
        self.copies = [
            [remote(slots.at[s], slots.at[4 + n], sems.at[n], peer) for n, peer in stage]
            for s, stage in enumerate(self.stages)
        ]

    def start(self, stage, value=None):
        if stage == 0:
            self.slots[0] = value
        for copy in self.copies[stage]:
            copy.start()

    def wait(self, stage):
        total = self.slots[stage].astype(f32)
        for copy, (n, _) in zip(self.copies[stage], self.stages[stage]):
            copy.wait()
            total = total + self.slots[4 + n].astype(f32)
        if stage < 3:
            self.slots[stage + 1] = total.astype(self.slots.dtype)
        return total


class SumSmall:
    def __init__(self, place, slots, sems):
        self.slots = slots
        t, w = place.t, place.w
        self.one = [remote(slots.at[0], slots.at[1 + i], sems.at[i], (t, (w + i) % 8)) for i in range(1, 8)]
        self.two = [remote(slots.at[1], slots.at[8 + i], sems.at[7 + i], ((t + i) % 4, w)) for i in range(1, 4)]

    def start(self, value):
        self.slots[0] = value
        for copy in self.one:
            copy.start()

    def turn(self):
        total = self.slots[0]
        for i, copy in enumerate(self.one):
            copy.wait()
            total = total + self.slots[2 + i]
        self.slots[1] = total
        for copy in self.two:
            copy.start()

    def finish(self):
        total = self.slots[1]
        for i, copy in enumerate(self.two):
            copy.wait()
            total = total + self.slots[9 + i]
        return total


SUM_SLOTS = 10


class Scatter:
    def __init__(self, place, grad, order, chain, bufs, sems):
        self.chain = chain
        self.p, self.grad, self.order, self.sems = place, grad, order, sems
        self.recv, self.s1, self.r1, self.r2, self.r3 = bufs
        self.s2 = self.s3 = self.s1.at[:, 0] if order == "xy" else self.s1.at[0]
        x, c, z, y = place.x, place.c, place.z, place.y
        self.core = remote(grad.at[:, 1 - c], self.recv, sems.at[0], place.other("c"))
        first, second = ("x", "y") if order == "xy" else ("y", "x")
        self.one = remote(self.s1, self.r1, sems.at[1], place.other(first))
        self.two = remote(self.s2, self.r2, sems.at[2], place.other(second))
        if not chain:
            self.three = [
                remote(self.s3.at[(z + s) % 4], self.r3.at[s - 1], sems.at[2 + s], place.along_z(s)) for s in (1, 2, 3)
            ]
            return
        self.hops = []
        for g in (1, 2, 3):
            down = (z >= 4 - g, (z + g) % 4, (z >= 3 - g) & (z <= 2), (z + g + 1) % 4, place.along_z(3))
            up = (z <= g - 1, (z - g + 4) % 4, (z <= g) & (z >= 1), (z - g + 3) % 4, place.along_z(1))
            self.hops.append([
                (remote(self.s3.at[g % 2 * 2 + d], self.r3.at[2 * g - 2 + d], sems.at[1 + 2 * g + d], peer), g % 2 * 2 + d, 2 * g - 2 + d, *rest)
                for d, (*rest, peer) in enumerate((down, up))
            ])

    def hop_start(self, hop):
        for copy, out, _, sends, block, _, _ in hop:
            @pl.when(sends)
            def _():
                self.s3[out] = self.recv[self.p.x, block, self.p.y].astype(bf16)
                copy.start()

    def hop_wait(self, hop):
        for copy, _, slot, sends, _, receives, block in hop:
            pl.when(sends)(copy.wait_send)

            @pl.when(receives)
            def _():
                copy.wait_recv()
                at = (self.p.x, block, self.p.y)
                self.recv[at] = self.recv[at] + self.r3[slot].astype(f32)

    def step(self, stage):
        x, c, z, y = self.p.x, self.p.c, self.p.z, self.p.y
        xy = self.order == "xy"
        if self.chain and stage > 3:
            self.hop_wait(self.hops[stage - 4])
            if stage < 6:
                self.hop_start(self.hops[stage - 3])
                return
            return self.recv[x, z, y]
        sums = self.recv
        if stage == 0:
            self.core.start()
        elif stage == 1:
            self.core.wait()
            sums[...] = sums[...] + self.grad[:, c]
            self.s1[...] = (sums[1 - x] if xy else sums[:, :, 1 - y]).astype(bf16)
            self.one.start()
        elif stage == 2:
            self.one.wait()
            if xy:
                sums[x] = sums[x] + self.r1[...].astype(f32)
                self.s2[...] = sums[x, :, 1 - y].astype(bf16)
            else:
                sums[:, :, y] = sums[:, :, y] + self.r1[...].astype(f32)
                self.s2[...] = sums[1 - x, :, y].astype(bf16)
            self.two.start()
        elif stage == 3:
            self.two.wait()
            sums[x, :, y] = sums[x, :, y] + self.r2[...].astype(f32)
            if self.chain:
                self.hop_start(self.hops[0])
                return
            self.s3[...] = sums[x, :, y].astype(bf16)
            for copy in self.three:
                copy.start()
        else:
            total = sums[x, z, y]
            for i, copy in enumerate(self.three):
                copy.wait()
                total = total + self.r3[i].astype(f32)
            return total


def scatter_bufs(rows, cols, order, chain):
    first = (4, 2, rows, cols) if order == "xy" else (2, 4, rows, cols)
    return [
        pltpu.VMEM((2, 4, 2, rows, cols), f32),
        pltpu.VMEM(first, bf16), pltpu.VMEM(first, bf16),
        pltpu.VMEM((4, rows, cols), bf16), pltpu.VMEM((6 if chain else 3, rows, cols), bf16),
    ]


ORDERS = ("yx", "xy")
SUM_ORDERS = (ORDERS,) * 4 + (("xy", "xy"),) * 3


VECTORS = 9


def layer_kernel(direct, W, groups, *refs):
    refs = list(refs)
    take = lambda n: [refs.pop(0) for _ in range(n)]
    count_s, count_f, tok, cot = take(4)
    if direct:
        sq, sp, fq, fp, up, dn, small = take(7)
    else:
        A, B, C, D, vec_in = take(5)
    result, gin = take(2)
    if direct:
        out_sq, out_sp, out_fq, out_fp, out_up, out_dn = take(6)
        out_small = take(10)
    else:
        gA, gB, gC, gD, gvec_out = take(5)
    arr, cots, leave, grecv, qkv_s, o_s, lse_s = take(7)
    vec, gvec, qkv, o, lse, stream, h2, wide, narrow = take(9)
    do, gleave = h2, cots
    dout, dh2 = wide.at[2], wide.at[3]
    if direct:
        A, B, C, D, gB, gC, gD = take(7)
        gA = gC
        vslots, eslots, lslots, wsems, vsems, esems, tsems, ssems = take(8)
        bufs = [take(5) for _ in range(14)]
    xsems, lsems = take(2)
    p = Place(W)
    t, w = p.t, p.w
    rank = t * 8 + w
    block_rows = W * TILE

    def of_peer(ref, m):
        return lambda peer: ref.at[m, peer * groups // W, pl.ds(peer * groups % W, groups)]

    of_cot = lambda m: lambda peer: cot.at[m, pl.ds(peer * groups, groups)]
    by_feature = lambda ref, m: lambda peer: ref.at[m, :, peer]
    by_sample = lambda ref, m: lambda peer: ref.at[m, pl.ds(peer * groups, groups)]
    cot_move = lambda m: Exchange(p, of_cot(m), by_feature(cots, m), xsems.at[m])
    first_move = lambda m: Exchange(p, of_peer(leave, m), by_feature(arr, m), xsems.at[2 + m])
    out_move = lambda m: Exchange(p, by_feature(leave, m), by_sample(result, m), xsems.at[4 + m])
    back_move = lambda m: Exchange(p, by_feature(gleave, m), by_sample(grecv, m), xsems.at[6 + m])
    gin_move = lambda m: pltpu.make_async_copy(grecv.at[m], gin.at[m], lsems.at[m])
    GA = GA2 = GB = GC = GD = SP = SQ0 = SQ2 = SQ3 = SB = SC = SD = ()
    if direct:
        lane_part = lambda ref, u, cols: ref.at[(slice(u, u + 1), *[slice(None)] * 5, cols)]
        GA, GA2, GB, GC, GD = (
            [Gather(p, lane_part(ref, u, cols), ORDERS[u], wsems.at[2 * n + u]) for u in (0, 1)]
            for n, (ref, cols) in enumerate(((A, LEFT), (A, RIGHT), (B, slice(0, 1024)), (C, slice(0, 1024)), (D, slice(0, 256))))
        )
        all_of = lambda size: (slice(0, size), slice(0, size))
        scatters = [
            Scatter(p, ref.at[(u, *[slice(None)] * 5, cols[u])], SUM_ORDERS[n][u], n > 3, bufs[2 * n + u], ssems.at[2 * n + u])
            for n, (ref, cols) in enumerate((
                (gA, (PART_P, PART_P)), (gA, PART_01), (gA, PART_2), (gA, PART_3),
                (gB, all_of(1024)), (gC, all_of(1024)), (gD, all_of(256)),
            )) for u in (0, 1)
        ]
        SP, SQ0, SQ2, SQ3, SB, SC, SD = (scatters[2 * n:2 * n + 2] for n in range(7))

    def pull(group, stage):
        for g in group:
            g.pull(stage)

    def push(group, stage):
        return [s.step(stage) for s in group]

    def serve(point, actions):
        for at, action in (actions.items() if direct else ()):
            if isinstance(point, int):
                if point == at:
                    action()
                continue

            @pl.when(point == at)
            def _():
                action()

    p.barrier(direct)
    if direct:
        at = (p.x, p.c, p.z, p.y)
        A[(0, *at)] = sq[:, 0:1024]
        A[(1, *at, slice(None), LEFT)] = sq[:, 1024:1536]
        A[(1, *at, slice(None), RIGHT)] = sp[...]
        pull(GA, 0)
        pull(GA2, 0)
        n, l = (lax.broadcasted_iota(jnp.int32, (16, 256), d) for d in (0, 1))
        short = (l < VECTORS * 16) & (l // 16 == n)
        long = (l >= VECTORS * 16) & (l < VECTORS * 16 + 64) & (n == VECTORS + rank // 8)
        spread = jnp.where(short | long, jnp.broadcast_to(small[...], (16, 256)), jnp.zeros((16, 256), bf16))
        l, j = (lax.broadcasted_iota(jnp.int32, (256, 512), d) for d in (0, 1))
        goal = jnp.where(l < VECTORS * 16, rank * 16 + l % 16, rank % 8 * 64 + l - VECTORS * 16)
        both = SumAll(p, vslots, vsems)
        both.start(0, mm(spread, (j == goal).astype(bf16)).astype(bf16))
        B[(0, *at)] = fq[:, 0:1024]
        B[(1, *at, slice(None), LEFT)] = fq[:, 1024:1536]
        B[(1, *at, slice(None), RIGHT)] = fp[...]
        for u in (0, 1):
            C[(u, *at)] = up[:, 1024 * u:1024 * u + 1024]
            D[(u, *at)] = dn[:, 256 * u:256 * u + 256]
    for ref in (gB, gC, gD):
        clear(ref)
    gvec[...] = jnp.zeros(gvec.shape, f32)
    if direct:
        pull(GA, 1)
        pull(GA2, 1)
        pull(GB, 0)
        pull(GA, 2)
        pull(GA2, 2)
        pull(GB, 1)
        both.wait(0)
        both.start(1)
        pull(GC, 0)
        pull(GA, 3)
        pull(GA2, 3)
        pull(GB, 2)
        pull(GC, 1)
        pull(GD, 0)
        both.wait(1)
        both.start(2)
        pull(GA, 4)
        pull(GA2, 4)
        pull(GB, 3)
        pull(GC, 2)
        pull(GD, 1)
        pull(GA, 5)
        both.wait(2)
        both.start(3)
        pull(GC, 3)
        pull(GD, 2)
        pull(GA2, 5)
        cot_move(0).start()
        rows = both.wait(3)
        for n in range(16):
            vec[n] = rows[n:n + 1]
        pull(GA, 6)
        pull(GA2, 6)
    else:
        cot_move(0).start()
        for n in range(16):
            vec[n] = vec_in[n:n + 1, :].astype(f32)
    row = lambda n: vec[n]
    everything = slice(None)
    whole_rows = lambda n: [(everything, n, lambda h: h)]
    half_of = lambda u: slice(256 * u, 256 * u + 256)
    moving = {
        0: lambda: pull(GD, 3),
        2: lambda: (pull(GB, 4), pull(GC, 4)),
        5: lambda: pull(GD, 4),
        15: lambda: pull(GB, 5),
    }

    def samples(m):
        extra = mask_lanes(512, count_s[0, m], 1)
        unit, _ = normed(tok[m].astype(f32))
        project((unit * row(0) + row(1)).astype(bf16), A, qkv_s.at[m])
        serve(m * 8, moving)

        def pairs(r):
            jobs = whole_rows(2 * r) + whole_rows(2 * r + 1)
            after = lambda phase: serve(m * 8 + 3 * r + 1 + phase, moving)
            attend(jobs, 512, extra, qkv_s.at[m], o_s.at[m], lse_s.at[m], wide, narrow, after)

        loop(2, pairs)
        branch = mm(o_s[m], out_proj(A)) + row(2)
        leave[m] = (tok[m].astype(f32) + branch).astype(bf16).reshape(leave.shape[1:])
        first_move(m).start()
        serve(m * 8 + 7, moving)

    def feature_blocks(body):
        def jobs_of(g, pairs):
            rows = pl.ds(g * block_rows, block_rows)
            return [(rows, n, lambda h: (h, everything, rows)) for n in pairs]

        if block_rows == 128:
            body([job for g in range(groups) for job in jobs_of(g, range(PAIRS))], block_rows)
        else:
            for g in range(groups):
                loop(PAIRS, lambda n: body(jobs_of(g, [n]), block_rows))

    def features(m):
        extra = mask_lanes(block_rows, count_f[0, m], TILE)
        first_move(m).wait()
        serve(m, {0: lambda: pull(GB, 6)})
        pl.when(m == 1)(lambda: cot_move(1).start())
        unit, _ = normed(flat(arr[m]).astype(f32))
        project((unit * row(3) + row(4)).astype(bf16), B, qkv.at[m])
        serve(m, {0: lambda: pull(GC, 5)})
        feature_blocks(lambda jobs, size: attend(jobs, size, extra, qkv.at[m], o.at[m], lse.at[m], wide, narrow))
        serve(m, {0: lambda: pull(GD, 5)})
        stream[m] = flat(arr[m]).astype(f32) + mm(o[m], out_proj(B)) + row(5)
        serve(m, {1: lambda: (pull(GC, 6), pull(GD, 6))})

    def feed(m):
        unit, _ = normed(stream[m])
        h2[...] = (unit * row(6) + row(7)).astype(bf16)
        cot_move(m).wait()

        def weights(n):
            cols = slice((n % 2) * 512, (n % 2) * 512 + 512)
            at = (n // 2, *[everything] * 5, cols)
            return at, C[at].reshape(512, 512), [D[u, n // 2, n % 2].reshape(512, 256) for u in (0, 1)]

        def enter(n):
            _, upw, dnw = weights(n)
            g16 = flat(cots[m])
            wide[0] = mm(h2[...], upw) + vec[VECTORS + n]
            wide[1] = mm_nt(g16[:, half_of(0)], dnw[0]) + mm_nt(g16[:, half_of(1)], dnw[1])

        def bend(n, i):
            part, b = slice(64 * i, 64 * i + 64), n % 2 * 2
            raised = wide[0, part]
            phi, e = gelu_parts(raised)
            narrow[b, part] = (raised * phi).astype(bf16)
            draised = (wide[1, part] * (phi + raised * e * (0.5 / jnp.pi) ** 0.5)).astype(bf16)
            narrow[b + 1, part] = draised
            return jnp.sum(draised.astype(f32).reshape(8, 8, 512), 0)

        def leave_chunk(n):
            at, upw, dnw = weights(n)
            b = n % 2 * 2

            def down(u):
                value = mm(narrow[b], dnw[u])
                dout[:, half_of(u)] = value if n == 0 else dout[:, half_of(u)] + value

            def back(u):
                value = mm_nt(narrow[b + 1], upw[half_of(u)])
                dh2[:, half_of(u)] = value if n == 0 else dh2[:, half_of(u)] + value

            def down_grad(u):
                put(gD, (u, n // 2, n % 2), mm_tn(narrow[b], flat(cots[m])[:, half_of(u)]))

            def up_grad():
                put(gC, at, mm_tn(h2[...], narrow[b + 1]))

            steps = [lambda f=f, u=u: f(u) for f in (down, back, down_grad) for u in (0, 1)]
            return steps + [up_grad, lambda: None]

        for n in range(5):
            if n < 4:
                enter(n)
            products = leave_chunk(n - 1) if n > 0 else [lambda: None] * 8
            total = jnp.zeros((8, 512), f32)
            for i in range(8):
                if n < 4:
                    total = total + bend(n, i)
                products[i]()
            if n < 4:
                gvec[VECTORS + n] += over_rows(total)
        leave[m] = (stream[m] + dout[...] + row(8)).astype(bf16).reshape(leave.shape[1:])
        pl.when(m == 0)(lambda: out_move(0).start())
        serve(m, {1: lambda: push(SC, 0)})
        cot16 = flat(cots[m]).astype(f32)
        gvec[8] += over_rows(cot16)
        unit, scale = normed(stream[m])
        dh = dh2[...]
        gvec[6] += over_rows(dh * unit)
        gvec[7] += over_rows(dh)
        stream[m] = cot16 + normed_back(dh, unit, scale, row(6))

    feature_steps = {
        0: lambda: push(SD, 0),
        1: lambda: push(SC, 1),
        2: lambda: push(SD, 1),
        5: lambda: push(SB, 0),
    }

    def features_back(m):
        extra = mask_lanes(block_rows, count_f[0, m], TILE)
        gy = stream[m].astype(bf16)
        put(gB, (1, Ellipsis, RIGHT), mm_tn(o[m], gy))
        gvec[5] += over_rows(gy.astype(f32))
        do[...] = mm_nt(gy, out_proj(B)).astype(bf16)
        serve(m * 3, feature_steps)
        here = qkv.at[m]
        feature_blocks(lambda jobs, size: attend_back(jobs, size, extra, here, o.at[m], lse.at[m], do, here, wide, narrow))
        serve(m * 3 + 1, feature_steps)
        unit, scale = normed(flat(arr[m]).astype(f32))
        dh = mm_nt(here[:, 0:1024], flat(B[0])) + mm_nt(here[:, 1024:1536], flat(B[1, ..., LEFT]))
        gleave[m] = (stream[m] + normed_back(dh, unit, scale, row(3))).astype(bf16).reshape(gleave.shape[1:])
        back_move(m).start()
        gvec[3] += over_rows(dh * unit)
        gvec[4] += over_rows(dh)
        h = (unit * row(3) + row(4)).astype(bf16)
        put(gB, 0, mm_tn(h, here[:, 0:1024]))
        put(gB, (1, Ellipsis, LEFT), mm_tn(h, here[:, 1024:1536]))
        serve(m * 3 + 2, feature_steps)

    def finish_c():
        out_up[:, 0:1024], out_up[:, 1024:2048] = push(SC, 6)

    def finish_d():
        out_dn[:, 0:256], out_dn[:, 256:512] = push(SD, 6)

    def finish_b():
        done = push(SB, 6)
        out_fq[:, 0:1024] = done[0]
        out_fq[:, 1024:1536] = done[1][:, LEFT]
        out_fp[...] = done[1][:, RIGHT]

    def fold(first, last):
        parts = [gvec[n][:, 128 * k:128 * k + 128] for n in range(first, last) for k in range(4)]
        pad = -len(parts) % 8
        return jnp.concatenate(parts + ([jnp.zeros((pad, 128), f32)] if pad else []), 0)

    early = SumSmall(p, eslots, esems) if direct else None
    late = SumSmall(p, lslots, tsems) if direct else None
    back_steps = {
        0: lambda: push(SC, 2),
        1: lambda: push(SB, 1),
        2: lambda: (push(SD, 2), push(SC, 3)),
        3: lambda: (push(SC, 4), out_move(1).start()),
        4: lambda: (push(SP, 0), push(SD, 3), early.start(fold(2, 13))),
        5: lambda: (push(SP, 1), push(SC, 5), push(SD, 4), push(SB, 2)),
        6: lambda: (push(SQ0, 0), finish_c(), push(SD, 5), push(SB, 3)),
        7: lambda: (push(SQ2, 0), push(SQ0, 1), push(SB, 4)),
        8: lambda: (push(SQ3, 0), push(SQ2, 1), finish_d(), push(SB, 5)),
        9: lambda: (push(SQ3, 1), push(SP, 2), push(SQ0, 2)),
        10: lambda: (push(SQ2, 2), early.turn()),
        11: lambda: (late.start(fold(0, 2)), push(SQ3, 2), push(SP, 3)),
        12: lambda: (push(SQ0, 3), push(SQ2, 3), finish_b()),
    }

    def samples_back(m):
        extra = mask_lanes(512, count_s[0, m], 1)
        back_move(m).wait()
        gy = flat(grecv[m])
        for u in (0, 1):
            put(gA, (u, *[everything] * 5, PART_P), mm_tn(o_s[m], gy[:, half_of(u)]))
        gvec[2] += over_rows(gy.astype(f32))
        do[...] = mm_nt(gy, out_proj(A)).astype(bf16)
        serve(m * 4, {4: back_steps[4]})
        unit, _ = normed(tok[m].astype(f32))
        h[...] = (unit * row(0) + row(1)).astype(bf16)
        here = qkv_s.at[m]

        def grads(pairs, parts):
            cols = [here[:, 512 * part + 128 * n:512 * part + 128 * n + 128] for part in range(3) for n in pairs]
            grad = mm_tn(h[...], jnp.concatenate(cols, 1))
            size = parts[0].stop - parts[0].start
            put(gA, (0, *[everything] * 5, parts[0]), grad[:, 0:size])
            put(gA, (1, *[everything] * 5, parts[1]), grad[:, size:])

        for n in range(PAIRS):
            attend_back(whole_rows(n), 512, extra, here, o_s.at[m], lse_s.at[m], do, here, wide, narrow)
            if n > 0:
                grads(*(((0, 1), PART_01), ((2,), PART_2), ((3,), PART_3))[n - 1])
            serve(m * 5 + n, {k: f for k, f in back_steps.items() if k in (n, n + 5)})

    def samples_norm(m):
        unit, _ = normed(tok[m].astype(f32))
        dh = mm_nt(qkv_s[m, :, 0:1024], flat(A[0])) + mm_nt(qkv_s[m, :, 1024:1536], flat(A[1, ..., LEFT]))
        wide[m] = dh
        serve(m, {0: back_steps[9]})
        gvec[0] += over_rows(dh * unit)
        gvec[1] += over_rows(dh)
        serve(m, {0: back_steps[10], 1: back_steps[11]})

    def samples_end(m):
        unit, scale = normed(tok[m].astype(f32))
        grecv[m] = (flat(grecv[m]).astype(f32) + normed_back(wide[m], unit, scale, row(0))).astype(bf16).reshape(grecv.shape[1:])
        gin_move(m).start()
        serve(m, {0: back_steps[12]})

    h = o.at[0]
    for phase in (samples, features, feed, features_back):
        loop(2, phase)
    clear(gA)
    if not direct:
        out_move(1).start()
    for phase in (samples_back, samples_norm, samples_end):
        loop(2, phase)
    if direct:
        late.turn()
        push(SQ3, 3)
        sums = early.finish()
        for u, part in enumerate(push(SP, 4)):
            out_sp[:, 256 * u:256 * u + 256] = part
        l, j = (lax.broadcasted_iota(jnp.int32, (128, 128), d) for d in (0, 1))

        def own(rows, start, size):
            return lax.dot_general(
                jnp.concatenate(rows, 0), (l == start + j).astype(f32), (((1,), (0,)), ((), ())),
                precision=lax.Precision.HIGHEST, preferred_element_type=f32,
            )[:, 0:size]

        def row_at(v, at):
            return over_rows(keep(lax.broadcasted_iota(jnp.int32, v.shape, 0) == at, v))

        zero = jnp.zeros((1, 128), f32)
        mine = own([row_at(sums, 4 * n + rank // 8) for n in range(7)] + [zero], rank % 8 * 16, 16)
        for n in range(7):
            out_small[2 + n][...] = mine[n:n + 1]
        long = row_at(sums, 4 * (7 + rank // 8) + rank % 8 // 2)
        out_small[VECTORS][...] = own([long] + [zero] * 7, rank % 2 * 64, 64)[0:1]
        sums = late.finish()
        mine = own([row_at(sums, 4 * n + rank // 8) for n in range(2)] + [zero] * 6, rank % 8 * 16, 16)
        for n in range(2):
            out_small[n][...] = mine[n:n + 1]
        for pairs, group in (((0, 1), SQ0), ((2,), SQ2), ((3,), SQ3)):
            done = jnp.concatenate(push(group, 4), 1)
            for i, (part, n) in enumerate((part, n) for part in range(3) for n in pairs):
                out_sq[:, 512 * part + 128 * n:512 * part + 128 * n + 128] = done[:, 128 * i:128 * i + 128]
    else:
        for n in range(VECTORS + 4):
            gvec_out[n:n + 1, :] = gvec[n]
        gvec_out[VECTORS + 4:, :] = jnp.zeros((3, 512), f32)
    for m in (0, 1):
        out_move(m).wait()
        gin_move(m).wait()


def copy_kernel(*refs):
    *refs, sems = refs
    n = len(refs) // 3
    moves = [
        [pltpu.make_async_copy(a, b, sems.at[i, k]) for k, (a, b) in enumerate(((refs[i], refs[2 * n + i]), (refs[2 * n + i], refs[n + i])))]
        for i in range(n)
    ]
    for enter, _ in moves:
        enter.start()
    for enter, leave in moves:
        enter.wait()
        leave.start()
    for _, leave in moves:
        leave.wait()


def shards(mesh, *args):
    (tokens, cotangent, sample_count, feature_count, sample_gain, sample_shift, sample_qkv, sample_proj, sample_bias,
     feature_gain, feature_shift, feature_qkv, feature_proj, feature_bias, mlp_gain, mlp_shift, up_weight, up_bias,
     down_weight, down_bias) = args
    T, W = mesh.shape["task"], mesh.shape["wide"]
    micro, _, length, _, width = tokens.shape
    groups = length // W // TILE
    direct = sample_qkv.shape[0] == TILE and T == 4 and W == 8
    axes = ("task", "wide")
    by_sample = (micro, groups, W, TILE, width)
    by_feature = (micro, W * groups, TILE, width)
    columns = lambda v: v.transpose(0, 1, 3, 2, 4)
    tok = columns(tokens).reshape(micro, length, width)
    cot = columns(cotangent).reshape(by_feature)
    vectors = (sample_gain, sample_shift, sample_bias, feature_gain, feature_shift, feature_bias, mlp_gain, mlp_shift, down_bias)
    V = pl.BlockSpec(memory_space=pltpu.VMEM)
    S = pl.BlockSpec(memory_space=pltpu.SMEM)
    H = pl.BlockSpec(memory_space=pl.ANY)
    sds = lambda shape, dtype=bf16: jax.ShapeDtypeStruct(shape, dtype)
    dma = lambda *shape: pltpu.SemaphoreType.DMA(shape)
    attention = [
        pltpu.VMEM((micro, length, 3 * width), bf16), pltpu.VMEM((micro, length, width), bf16), pltpu.VMEM((micro, HEADS, 1, length), f32),
    ]
    square, tall = (2, *SPLIT, TILE, 1024), (2, *SPLIT, 64, 256)
    scratch = [pltpu.VMEM(by_sample, bf16)] * 3 + [
        pltpu.VMEM(by_feature, bf16), *attention, pltpu.VMEM((16, 1, width), f32), pltpu.VMEM((16, 1, width), f32),
        *attention, pltpu.VMEM((micro, length, width), f32), pltpu.VMEM((length, width), bf16),
        pltpu.VMEM((4, length, width), f32), pltpu.VMEM((4, length, width), bf16),
    ]
    matrices = (sample_qkv, sample_proj, feature_qkv, feature_proj, up_weight, down_weight)
    outs = [sds(by_feature), sds(by_feature)]
    counts = (sample_count.T, feature_count.T)
    if direct:
        small = jnp.concatenate([*vectors, up_bias, jnp.zeros(48, bf16)]).reshape(1, 256)
        ins = (*matrices, small)
        outs += [sds(v.shape, f32) for v in matrices] + [sds((1, v.shape[0]), f32) for v in (*vectors, up_bias)]
        scratch += [pltpu.VMEM(square, bf16)] * 3 + [pltpu.VMEM(tall, bf16)] + [pltpu.VMEM(square, f32)] * 2 + [pltpu.VMEM(tall, f32)]
        scratch += [pltpu.VMEM((SUM_SLOTS, 16, width), bf16), pltpu.VMEM((12, 48, 128), f32), pltpu.VMEM((12, 8, 128), f32)]
        scratch += [dma(10, 9, 2), dma(6, 2), dma(11, 2), dma(11, 2), dma(14, 9, 2)]
        sizes = ((TILE, (256, 256)), (TILE, (384, 384)), (TILE, (256, 128)), (TILE, (128, 256)),
                 (TILE, (1024, 1024)), (TILE, (1024, 1024)), (64, (256, 256)))
        for (rows, cols), orders in zip(sizes, SUM_ORDERS):
            for u in (0, 1):
                scratch += scatter_bufs(rows, cols[u], orders[u], cols[u] == 1024 or rows > TILE)
    else:
        gather = lambda v: lax.all_gather(v, axes, axis=0, tiled=True)
        sq, sp, fq, fp, up, dn = map(gather, matrices)
        pair = lambda q, o: jnp.stack([q[:, 0:1024], jnp.concatenate([q[:, 1024:], o], 1)]).reshape(square)
        C = jnp.stack([up[:, 0:1024], up[:, 1024:]]).reshape(square)
        D = jnp.stack([dn[:, 0:256], dn[:, 256:]]).reshape(tall)
        rest = [gather(up_bias).reshape(4, width), jnp.zeros((3, width), bf16)]
        ins = (pair(sq, sp), pair(fq, fp), C, D, jnp.concatenate([jnp.stack([gather(v) for v in vectors]), *rest], 0))
        outs += [sds(square, f32)] * 3 + [sds(tall, f32), sds((16, width), f32)]
    done = pl.pallas_call(
        lambda *refs: layer_kernel(direct, W, groups, *refs), name="layer",
        in_specs=[S, S, V, H] + [V] * len(ins), out_specs=[H, H] + [V] * (len(outs) - 2), out_shape=outs,
        scratch_shapes=scratch + [dma(8, W, 2), dma(2)],
        compiler_params=pltpu.CompilerParams(collective_id=1, has_side_effects=True, vmem_limit_bytes=63 * MIB + MIB * 7 // 8),
    )(*counts, tok, cot, *ins)
    if direct:
        done = pl.pallas_call(
            copy_kernel, name="hand_out", in_specs=[H] * len(outs), out_specs=[H] * len(outs), out_shape=outs,
            scratch_shapes=[pltpu.VMEM(v.shape, v.dtype) for v in outs] + [dma(len(outs), 2)],
        )(*done)
    restore = lambda v: columns(v.reshape(micro, 1, 1, length, width))
    output, input_grad = restore(done[0]), restore(done[1])
    if direct:
        g_sq, g_sp, g_fq, g_fp, g_up, g_dn = done[2:8]
        g = [v.reshape(-1) for v in done[8:18]]
    else:
        gA, gB, gC, gD, gv = done[2:7]
        two = lambda v: v.reshape(2, -1, v.shape[-1])
        joined = lambda v: jnp.concatenate([two(v)[0], two(v)[1]], 1)
        b = joined(gB)
        held = {}
        for pairs, parts in (((0, 1), PART_01), ((2,), PART_2), ((3,), PART_3)):
            both = jnp.concatenate([two(gA)[u][:, parts[u]] for u in (0, 1)], 1)
            for i, place in enumerate((part, n) for part in range(3) for n in pairs):
                held[place] = both[:, 128 * i:128 * i + 128]
        proj = [two(gA)[u][:, PART_P] for u in (0, 1)]
        a = jnp.concatenate([held[part, n] for part in range(3) for n in range(PAIRS)] + proj, 1)
        scatter = lambda v: lax.psum_scatter(v, axes, scatter_dimension=0, tiled=True)
        g_sq, g_sp, g_fq, g_fp, g_up, g_dn = map(scatter, (a[:, :1536], a[:, 1536:], b[:, :1536], b[:, 1536:], joined(gC), joined(gD)))
        g = [scatter(gv[n]) for n in range(VECTORS)] + [scatter(gv[VECTORS:VECTORS + 4].reshape(-1))]
    return (output, input_grad, g[0], g[1], g_sq, g_sp, g[2], g[3], g[4], g_fq, g_fp, g[5], g[6], g[7], g_up, g[9], g_dn, g[8])


def solution(mesh):
    rows = P(("task", "wide"))
    table = P(("task", "wide"), None)
    data = P(None, "task", None, "wide", None)
    params = (rows, rows, table, table, rows, rows, rows, table, table, rows, rows, rows, table, rows, table, rows)
    counts = P(None, "task")

    def run(*args):
        return shards(mesh, *args)

    return jax.shard_map(
        run, mesh=mesh, in_specs=(data, data, counts, counts) + params, out_specs=(data, data) + params, check_vma=False
    )
```
